32 devices in a mesh: batch: 2 (over core), grid: 16 (over z, y, x).
Axes of the slice: x: 2, y: 2, z: 4, core: 2. Of those that a mesh axis runs over, the one named last changes fastest.
Arguments:
- inputs: bfloat16 [16, 64, 64, 512], P('batch', 'grid'), may hold values from -17 to 17
- cotangent: bfloat16 [16, 64, 64, 512], P('batch', 'grid'), may hold values from -6 to 6
- dataset_ids: int32 [16], P('batch'), may hold values from 0 to 11
- channel_masks: int32 [12, 4], replicated, may hold values 0 or 1
- sample_counts: int32 [12], replicated, may hold values from 4 to 16
- norm1_gain: float32 [512], replicated, may hold values from 0.25 to 1.75
- norm1_bias: float32 [512], replicated, may hold values from -1 to 1
- spec_w1: bfloat16 [2, 8, 64, 64], replicated, may hold values from -0.5 to 0.5
- spec_b1: float32 [2, 512], replicated, may hold values from -1.5 to 1.5
- spec_w2: bfloat16 [2, 8, 64, 64], replicated, may hold values from -0.75 to 0.75
- spec_b2: float32 [2, 512], replicated, may hold values from -1.5 to 1.5
- norm2_gain: float32 [512], replicated, may hold values from 0.25 to 1.75
- norm2_bias: float32 [512], replicated, may hold values from -1 to 1
- mlp_in: bfloat16 [512, 2048], replicated, may hold values from -0.25 to 0.25
- mlp_in_bias: float32 [2048], replicated, may hold values from -1.5 to 1.5
- mlp_out: bfloat16 [2048, 512], replicated, may hold values from -0.25 to 0.25
- mlp_out_bias: float32 [512], replicated, may hold values from -1.5 to 1.5
Outputs:
- activations: bfloat16 [16, 64, 64, 512], P('batch', 'grid')
- input_grad: float32 [16, 64, 64, 512], P('batch', 'grid')
- norm1_gain_grad: float32 [512], replicated
- norm1_bias_grad: float32 [512], replicated
- spec_w1_grad: float32 [2, 8, 64, 64], replicated
- spec_b1_grad: float32 [2, 512], replicated
- spec_w2_grad: float32 [2, 8, 64, 64], replicated
- spec_b2_grad: float32 [2, 512], replicated
- norm2_gain_grad: float32 [512], replicated
- norm2_bias_grad: float32 [512], replicated
- mlp_in_grad: float32 [512, 2048], replicated
- mlp_in_bias_grad: float32 [2048], replicated
- mlp_out_grad: float32 [2048, 512], replicated
- mlp_out_bias_grad: float32 [512], replicated
The draws below stay inside these ranges and needn't reach their ends.
All inputs are finite; a program needn't handle non-finite values.
Results may differ from the reference program's by a relative error of at most 0.017.
The reference program's roundings to bfloat16 on the way count: a program that leaves them out, or rounds other values in their place, can miss the bound.
Values may be sent and summed in bfloat16 or wider, within the bound.
A program may use at most 192 MiB of HBM per device.

```python
import math
import jax
import jax.numpy as jnp
from jax import lax

D = 512
BLOCKS = 8
MLP = 2048
MODES = 32
GRID_H = 64
GRID_W = 64
GROUPS = 4
DATASETS = 12
BSIZE = 64
ITEMS = 16


def draw_inputs(key, part):
    key = jax.random.fold_in(key, 11)
    key_vals, key_chan, key_cell = jax.random.split(key, 3)
    chan_scale = jnp.exp(jax.random.uniform(key_chan, (D,), jnp.float32, math.log(0.3), math.log(3.0)))
    values = jax.random.truncated_normal(key_vals, -4.0, 4.0, (ITEMS, GRID_H, GRID_W, D), jnp.float32)
    cell_scale = jnp.exp(jax.random.uniform(key_cell, (ITEMS, GRID_H, GRID_W, 1), jnp.float32, math.log(0.7), math.log(1.4)))
    return (values * chan_scale * cell_scale).astype(jnp.bfloat16)


def with_ends(result, rng, least, largest):
    index_at = [jax.random.randint(jax.random.fold_in(rng, axis), (), 0, length) for axis, length in enumerate(result.shape)]
    longest = result.shape.index(max(result.shape))
    beside = index_at[:longest] + [(index_at[longest] + 1) % result.shape[longest]] + index_at[longest + 1:]
    return result.at[tuple(index_at)].set(least).at[tuple(beside)].set(largest)


def steps_of(own_key, dims, pieces, smallest, high):
    factor_of, own = 1.0, jax.random.fold_in(own_key, 6)
    for position, parts in pieces:
        heights = jnp.exp(jax.random.uniform(jax.random.fold_in(own, position), (parts,), jnp.float32, smallest / len(pieces), high / len(pieces)))
        factor_of = factor_of * jnp.repeat(heights, dims[position] // parts).reshape([-1 if axis == position else 1 for axis in range(len(dims))])
    return factor_of


def gaussian(own_key, shape, scale, most, pieces=(), kind=jnp.bfloat16):
    loudness = steps_of(own_key, shape, pieces, -0.22, 0.18) if pieces else 1.0
    result = jax.random.normal(own_key, shape, jnp.float32) * scale * loudness
    return jnp.minimum(jnp.maximum(result, -most), most).astype(kind)


def setup_inputs(seed: int = 0) -> dict:
    seeds = jax.random.split(jax.random.key(seed), 18)
    inputs = draw_inputs(jax.random.fold_in(seeds[17], 71), 0)
    cotangent = gaussian(seeds[1], (ITEMS, GRID_H, GRID_W, D), 1.0, 6.0, ((0, 2), (1, 16)))
    dataset_ids = with_ends(jax.random.randint(seeds[2], (ITEMS,), 0, DATASETS), jax.random.fold_in(seeds[2], 1), 0, DATASETS - 1).astype(jnp.int32)
    channel_masks = with_ends((jax.random.randint(seeds[3], (DATASETS, GROUPS), 0, 4) < 3).astype(jnp.int32), jax.random.fold_in(seeds[3], 1), 0, 1)
    sample_counts = with_ends(jax.random.randint(seeds[4], (DATASETS,), 4, 17), jax.random.fold_in(seeds[4], 1), 4, 16).astype(jnp.int32)
    norm1_gain = jnp.clip(1.0 + 0.15 * jax.random.normal(seeds[5], (D,), jnp.float32), 0.25, 1.75)
    norm1_bias = gaussian(seeds[6], (D,), 0.2, 1.0, (), jnp.float32)
    spec_w1 = gaussian(seeds[7], (2, BLOCKS, BSIZE, BSIZE), (2 * BSIZE) ** -0.5, 0.5)
    spec_b1 = gaussian(seeds[8], (2, D), 0.3, 1.5, (), jnp.float32)
    spec_w2 = gaussian(seeds[9], (2, BLOCKS, BSIZE, BSIZE), BSIZE ** -0.5, 0.75)
    spec_b2 = gaussian(seeds[10], (2, D), 0.3, 1.5, (), jnp.float32)
    norm2_gain = jnp.clip(1.0 + 0.15 * jax.random.normal(seeds[11], (D,), jnp.float32), 0.25, 1.75)
    norm2_bias = gaussian(seeds[12], (D,), 0.2, 1.0, (), jnp.float32)
    mlp_in = gaussian(seeds[13], (D, MLP), D ** -0.5, 0.25)
    mlp_in_bias = gaussian(seeds[14], (MLP,), 0.3, 1.5, (), jnp.float32)
    mlp_out = gaussian(seeds[15], (MLP, D), (MLP // 4) ** -0.5, 0.25)
    mlp_out_bias = gaussian(seeds[16], (D,), 0.3, 1.5, (), jnp.float32)
    return {"inputs": inputs, "cotangent": cotangent, "dataset_ids": dataset_ids, "channel_masks": channel_masks, "sample_counts": sample_counts, "norm1_gain": norm1_gain, "norm1_bias": norm1_bias, "spec_w1": spec_w1, "spec_b1": spec_b1, "spec_w2": spec_w2, "spec_b2": spec_b2, "norm2_gain": norm2_gain, "norm2_bias": norm2_bias, "mlp_in": mlp_in, "mlp_in_bias": mlp_in_bias, "mlp_out": mlp_out, "mlp_out_bias": mlp_out_bias}


EPSILON = 1e-06
SHRINK = 0.1
PRECISE = lax.Precision.HIGHEST

@jax.custom_vjp
def low(v):
    return lax.optimization_barrier(v.astype(jnp.bfloat16)).astype(jnp.float32)

@jax.custom_vjp
def low_back(v):
    return v

def low_keep(v):
    return (low(v), None)

def low_pass(kept, grad):
    return (grad,)

def back_keep(v):
    return (v, None)

def back_low(kept, grad):
    return (low(grad),)
low.defvjp(low_keep, low_pass)
low_back.defvjp(back_keep, back_low)

def layer_norm(values, gain_vec, bias_vec):
    average = lax.optimization_barrier(jnp.mean(values, axis=-1, keepdims=True))
    centred = values - average
    variance = lax.optimization_barrier(jnp.mean(centred * centred, axis=-1, keepdims=True))
    return centred * lax.rsqrt(variance + EPSILON) * gain_vec + bias_vec

def gelu_exact(values):
    return jax.nn.gelu(values, approximate=False)

def smooth_shrink(values):
    return values - SHRINK * jnp.tanh(values / SHRINK)

def col_table(grid_cols, mode_count):
    col_idx = jnp.arange(grid_cols, dtype=jnp.int32)[:, None]
    mode_idx = jnp.arange(mode_count, dtype=jnp.int32)[None, :]
    angles = (col_idx * mode_idx % grid_cols).astype(jnp.float32) * (2.0 * math.pi / grid_cols)
    return jnp.stack([jnp.cos(angles), -jnp.sin(angles)], axis=1) * (1.0 / math.sqrt(grid_cols))

def inverse_col_table(col_tab):
    mode_count = col_tab.shape[2]
    doubling = jnp.where(jnp.arange(mode_count, dtype=jnp.int32) == 0, 1.0, 2.0).astype(jnp.float32)
    return jnp.transpose(col_tab, (2, 1, 0)) * doubling[:, None, None]

def row_table(height, mode_count):
    mode_idx = jnp.arange(mode_count, dtype=jnp.int32)
    frequency = jnp.where(mode_idx < mode_count // 2, mode_idx, height - mode_count + mode_idx)
    row_idx = jnp.arange(height, dtype=jnp.int32)
    angles = (frequency[:, None] * row_idx[None, :] % height).astype(jnp.float32) * (2.0 * math.pi / height)
    cosine = jnp.cos(angles)
    sine_vals = jnp.sin(angles)
    real_row = jnp.stack([cosine, sine_vals], axis=-1)
    imag_row = jnp.stack([-sine_vals, cosine], axis=-1)
    return jnp.stack([real_row, imag_row], axis=1) * (1.0 / math.sqrt(height))

def mix_modes(values, weights, bias_vec):
    split_vals = values.reshape(values.shape[:-1] + (BLOCKS, BSIZE))
    real_in = split_vals[..., 0, :, :]
    imag_in = split_vals[..., 1, :, :]
    real_out = jnp.einsum('...kb,kbc->...kc', real_in, weights[0], precision=PRECISE) - jnp.einsum('...kb,kbc->...kc', imag_in, weights[1], precision=PRECISE)
    imag_out = jnp.einsum('...kb,kbc->...kc', real_in, weights[1], precision=PRECISE) + jnp.einsum('...kb,kbc->...kc', imag_in, weights[0], precision=PRECISE)
    joined = jnp.stack([real_out, imag_out], axis=-3) + bias_vec.reshape(2, BLOCKS, BSIZE)
    return joined.reshape(values.shape)

def forward(item_val, live_row, param_set, col_tab, inv_tab, row_tab):
    gain_one, bias_one, w_first, b_first, w_second, b_second, gain_two, bias_two, w_in, b_in, w_out, b_out = param_set
    normed = layer_norm(item_val, gain_one, bias_one)
    col_spec = low(low_back(jnp.einsum('hwd,wrq->hqrd', normed, col_tab, precision=PRECISE)))
    mode_vals = low(jnp.einsum('hqrd,pshr->pqsd', col_spec, row_tab, precision=PRECISE))
    mixed_one = low_back(mix_modes(mode_vals, w_first, b_first))
    act_one = low(gelu_exact(mixed_one))
    mixed_two = low_back(mix_modes(act_one, w_second, b_second))
    shrunk = low(smooth_shrink(mixed_two))
    row_back = low(low_back(jnp.einsum('pqrd,prhs->hqsd', shrunk, row_tab, precision=PRECISE)))
    spatial = jnp.einsum('hqrd,qrw->hwd', row_back, inv_tab, precision=PRECISE)
    residual = item_val + spatial * live_row
    normed_two = low(layer_norm(residual, gain_two, bias_two))
    hidden = low_back(jnp.einsum('hwd,df->hwf', normed_two, w_in, precision=PRECISE) + b_in)
    act_two = low(gelu_exact(hidden))
    branch = low_back(jnp.einsum('hwf,fd->hwd', act_two, w_out, precision=PRECISE) + b_out)
    return residual + branch

def add_pair(first_arr, second_arr):
    return first_arr + second_arr

def reference(inputs, cotangent, dataset_ids, channel_masks, sample_counts, norm1_gain, norm1_bias, spec_w1, spec_b1, spec_w2, spec_b2, norm2_gain, norm2_bias, mlp_in, mlp_in_bias, mlp_out, mlp_out_bias):
    col_tab = col_table(GRID_W, MODES)
    inv_tab = inverse_col_table(col_tab)
    row_tab = row_table(GRID_H, MODES)
    param_set = (norm1_gain, norm1_bias, spec_w1.astype(jnp.float32), spec_b1, spec_w2.astype(jnp.float32), spec_b2, norm2_gain, norm2_bias, mlp_in.astype(jnp.float32), mlp_in_bias, mlp_out.astype(jnp.float32), mlp_out_bias)
    group_live = channel_masks[dataset_ids].astype(jnp.float32)
    chan_live = jnp.repeat(group_live, D // GROUPS, axis=1)
    item_weight = sample_counts[dataset_ids].astype(jnp.float32) / 8.0

    def one_item(totals, packed):
        item_val, cot_val, live_row, item_scale = packed

        def run(value_in, params_in):
            return forward(value_in, live_row, params_in, col_tab, inv_tab, row_tab)
        out_val, pull_back = jax.vjp(run, item_val.astype(jnp.float32), param_set)
        grad_item, grad_params = pull_back(cot_val.astype(jnp.float32) * item_scale)
        totals = jax.tree.map(add_pair, totals, grad_params)
        return (totals, (out_val.astype(jnp.bfloat16), grad_item))
    start = jax.tree.map(jnp.zeros_like, param_set)
    totals, (activations, input_grad) = lax.scan(one_item, start, (inputs, cotangent, chan_live, item_weight))
    return (activations, input_grad, totals[0], totals[1], totals[2], totals[3], totals[4], totals[5], totals[6], totals[7], totals[8], totals[9], totals[10], totals[11])
```

```python
import functools
import math

import jax
import jax.numpy as jnp
import numpy as np
from jax import lax
from jax.experimental import pallas as pl
from jax.experimental.pallas import tpu as pltpu
from jax.sharding import PartitionSpec as P

BLOCKS = 8
MODES = 32
BSIZE = 64
EPSILON = 1e-06
SHRINK = 0.1
MESH = pl.DeviceIdType.MESH
F32 = jnp.float32
BF16 = jnp.bfloat16
CELLS = 512
TILE = 16
COPY = 32
FT = 512


def sizes_of(items, rows, cols, feats, hidden, grid):
    sz = type("Sizes", (), {})()
    sz.items, sz.rows, sz.cols, sz.feats, sz.hidden, sz.grid = items, rows, cols, feats, hidden, grid
    sz.own = MODES // grid
    sz.height = rows * grid
    sz.item_cells = rows * cols
    sz.sub_items = 16 // (rows * sz.own * 2)
    sz.sub_cells = sz.sub_items * sz.item_cells
    sz.subs = CELLS // sz.sub_cells
    sz.chunk_items = sz.subs * sz.sub_items
    sz.chunks = items // sz.chunk_items
    sz.sub_modes = sz.sub_items * sz.own * MODES
    sz.modes = sz.subs * sz.sub_modes
    return sz


def halves(table):
    high = table.astype(BF16)
    low = (table - high.astype(np.float64)).astype(BF16)
    return np.stack([high, low])


def tables(sz):
    its, rows, own, cols, grid = sz.sub_items, sz.rows, sz.own, sz.cols, sz.grid
    w = np.arange(cols)
    q = np.arange(MODES)
    angle = 2 * np.pi * (np.outer(q, w) % cols) / cols
    col = np.stack([np.cos(angle), -np.sin(angle)], axis=1) / math.sqrt(cols)
    lines = its * rows
    eye = np.eye(lines)

    def placed(tab):
        tab = tab.reshape(grid, own, 2, cols)
        big = np.einsum("gqrw,lm->glqrmw", tab, eye)
        return big.reshape(grid * 16, lines * cols)

    first = placed(col)
    p = np.where(q < MODES // 2, q, sz.height - MODES + q)
    h = np.arange(sz.height)
    angle = 2 * np.pi * (np.outer(p, h) % sz.height) / sz.height
    cosine, sine = np.cos(angle), np.sin(angle)
    row = np.stack([np.stack([cosine, sine], -1), np.stack([-sine, cosine], -1)], 1) / math.sqrt(sz.height)
    row = row.reshape(MODES, 2, grid, rows, 2)
    big = np.einsum("psghr,ij,qk->siqpgjhkr", row, np.eye(its), np.eye(own))
    big = big.reshape(2 * sz.sub_modes, grid * 16)
    return [halves(t) for t in (first, first.T, big, big.T)]


def dot(a, b):
    return jnp.dot(a, b, preferred_element_type=F32)


def dot_nt(a, b):
    return lax.dot_general(a, b, (((1,), (1,)), ((), ())), preferred_element_type=F32)


def dot_tn(a, b):
    return lax.dot_general(a, b, (((0,), (0,)), ((), ())), preferred_element_type=F32)


def split(v):
    high = v.astype(BF16)
    return high, (v - high.astype(F32)).astype(BF16)


CDF = (
    0.797884941492634, 0.03633308439449127, -3.259472654998994e-05, -5.530632529808752e-05, 3.964774886835927e-06,
    -1.3226642974616402e-07, 1.756281964154736e-09,
)


def gelu_parts(v):
    square = v * v
    inner = jnp.minimum(square, 30.0)
    q = CDF[6] * inner + CDF[5]
    for coef in CDF[4::-1]:
        q = q * inner + coef
    cdf = 0.5 + 0.5 * jnp.tanh(v * q)
    pdf = jnp.exp2(square * (-0.5 * math.log2(math.e))) * (1.0 / math.sqrt(2.0 * math.pi))
    return v * cdf, cdf + v * pdf


def moments(v):
    centred = v - jnp.mean(v, axis=-1, keepdims=True)
    scale = lax.rsqrt(jnp.mean(centred * centred, axis=-1, keepdims=True) + EPSILON)
    return centred * scale, scale


def pull_norm(grad, xhat, scale, gain):
    gy = grad * gain
    return (gy - jnp.mean(gy, -1, keepdims=True) - xhat * jnp.mean(gy * xhat, -1, keepdims=True)) * scale


def eight_rows(v):
    return jnp.sum(v.reshape(v.shape[0] // 8, 8, v.shape[1]), axis=0)


GAIN1, BIAS1, SB1, SB2, GAIN2, BIAS2, BOUT, BIN = 0, 1, 2, 4, 6, 7, 8, 9


def tiled(count, body):
    size = min(count, COPY)

    @pl.loop(0, count // size, unroll=min(4, count // size))
    def _(t):
        body(t * size, size)


def each_tile(rows):
    return pl.loop(0, rows // TILE, unroll=rows // TILE)


def landing_rows(rows, bits):
    total = 0
    for _ in range(bits):
        rows = rows // 2 if rows % 32 == 0 else rows
        total += rows
    return total


class Pieces:
    def __init__(self, source, target, rows, send_sem, recv_sem, device):
        self.source, self.target, self.rows, self.device = source, target, rows, device
        self.send_sem, self.recv_sem = send_sem, recv_sem

    def part(self, at):
        return pltpu.make_async_remote_copy(
            src_ref=self.source.at[at], dst_ref=self.target.at[at], send_sem=self.send_sem, recv_sem=self.recv_sem,
            device_id=self.device, device_id_type=MESH,
        )

    def start(self):
        size = max(16, self.rows // 8)

        @pl.loop(0, self.rows // size)
        def _(k):
            self.part(pl.ds(pl.multiple_of(k * size, 16), size)).start()

    def wait_send(self):
        self.part(pl.ds(0, self.rows)).wait_send()

    def wait_recv(self):
        self.part(pl.ds(0, self.rows)).wait_recv()


class Reducer:
    def __init__(self, acc, stages, landing, near, send_sems, recv_sems, order, index):
        self.acc, self.stages, self.landing, self.near = acc, stages, landing, near
        self.send_sems, self.recv_sems = send_sems, recv_sems
        self.steps = []
        size, off, land = acc.shape[0], 0, 0
        for axis, bit in order:
            side = lax.rem(index[axis] // 2**bit, 2)
            partner = {axis: index[axis] + (1 - 2 * side) * 2**bit}
            halving = size % 32 == 0
            if halving:
                size = size // 2
                away, off = off + (1 - side) * size, off + side * size
            else:
                away = off
            self.steps.append((halving, size, away, off, land, partner))
            land += size
        self.off, self.size = off, size
        self.back = [k for k in reversed(range(1, len(order))) if self.steps[k][0]]

    def at(self, off, size):
        return pl.ds(pl.multiple_of(off, 16), size)

    def stage(self, k):
        halving, size, away, off, land, partner = self.steps[k]
        if not halving:
            return self.near(off - self.steps[0][3], size)
        return self.stages[0] if k == 0 else self.stages[1].at[pl.ds(land - self.steps[0][1], size)]

    def copy(self, k):
        halving, size, away, off, land, partner = self.steps[k]
        return Pieces(
            self.stage(k), self.landing.at[pl.ds(land, size)], size, self.send_sems.at[k], self.recv_sems.at[k], partner
        )

    def start(self, k):
        halving, size, away, off, land, partner = self.steps[k]

        stage = self.stage(k)

        def body(o, n):
            stage[pl.ds(o, n), :] = self.acc[self.at(away + o, n), :].astype(BF16)

        tiled(size, body)
        self.copy(k).start()

    def finish(self, k):
        halving, size, away, off, land, partner = self.steps[k]
        self.copy(k).wait_recv()
        if not halving:
            self.copy(k).wait_send()
        stage = self.stage(k)

        def body(o, n):
            at = self.at(off + o, n)
            mine = self.acc[at, :] if halving else stage[pl.ds(o, n), :].astype(F32)
            self.acc[at, :] = mine + self.landing[pl.ds(land + o, n), :].astype(F32)

        tiled(size, body)

    def begin_back(self):
        first = self.steps[0][3]

        def body(o, n):
            at = self.at(self.off + o, n)
            self.near(self.off - first + o, n)[...] = self.acc[at, :].astype(BF16)

        tiled(self.size, body)

    def back_copy(self, i):
        halving, size, away, off, land, partner = self.steps[self.back[i]]
        part = self.near(off - self.steps[0][3], size)
        sem = len(self.steps) + i
        return Pieces(part, part, size, self.send_sems.at[sem], self.recv_sems.at[sem], partner)

    def ticks(self):
        count, back = len(self.steps), len(self.back)

        def first():
            self.start(0)

        def forth(k):
            self.finish(k)
            if k + 1 < count:
                self.start(k + 1)
            else:
                self.begin_back()
                self.back_copy(0).start()

        def home(i):
            self.back_copy(i).wait_recv()
            if i + 1 < back:
                self.back_copy(i + 1).start()

        return (
            [first]
            + [functools.partial(forth, k) for k in range(count)]
            + [functools.partial(home, i) for i in range(back)]
        )

    def wait_sent(self):
        for k, step in enumerate(self.steps):
            if step[0]:
                self.copy(k).wait_send()
        for i in range(len(self.back)):
            self.back_copy(i).wait_send()


def kernel(
    sz, batch_bits, grid_bits,
    ids, masks, counts,
    x_hbm, cot_hbm, gain1, bias1, gain2, bias2, sw1, sb1, sw2, sb2, b_in, b_out,
    t_f, t_b, t_rf, t_rb, win_hbm, wout_hbm,
    act_hbm, ig_hbm, near_hbm, dspec_out, dvec_out,
    x_v, cot_v, w_in, w_out, send_a, recv_a, send_b, recv_b, gres,
    spec, act1, slope1, slope2, w1, w2, dw1, dw2,
    n2, n2t, gb, gbt, act_s, gh_s, live, weight,
    dm_acc, dm_land, late_acc, late_stage, late_land, late_split, late_parts, late_near, late_far, dvec, sums, hid_s, pul_s, n1_send, n1_recv,
    sem_x, sem_cot, sem_w, sem_out, sem_ig, sem_dm, send_sems, recv_sems,
    dm_send, dm_recv, late_send, late_recv, n1_ssem, n1_rsem,
):
    grid, feats = sz.grid, sz.feats
    chunks, subs = sz.chunks, sz.subs
    me = lax.axis_index("grid")
    index = {"batch": lax.axis_index("batch"), "grid": me}
    hi_v, lo_v = n2, gb
    modes = sz.modes
    groups = feats // 128
    mix_rows = 4 * groups * BSIZE
    blocks = sz.hidden // FT
    order = [("batch", b) for b in range(batch_bits)] + [("grid", b) for b in range(grid_bits)]
    swapped = list(order)
    if grid_bits > 1:
        swapped[batch_bits], swapped[batch_bits + 1] = swapped[batch_bits + 1], swapped[batch_bits]

    for c in range(chunks):
        pltpu.make_async_copy(x_hbm.at[c], x_v.at[c], sem_x.at[c]).start()
    for c in range(chunks):
        pltpu.make_async_copy(cot_hbm.at[c], cot_v.at[c], sem_cot.at[c]).start()
    load_win = pltpu.make_async_copy(win_hbm, w_in, sem_w.at[0])
    load_wout = pltpu.make_async_copy(wout_hbm, w_out, sem_w.at[1])
    load_win.start()
    load_wout.start()

    barrier = pltpu.get_barrier_semaphore()

    def other(k):
        batch = 2**batch_bits
        b = lax.rem(index["batch"] + k // grid, batch)
        g = lax.rem(me + lax.rem(k, grid), grid)
        return {"batch": b, "grid": g}

    everyone = 2**batch_bits * grid
    my_place = index["batch"] * grid + me

    @pl.loop(1, everyone)
    def _(k):
        pl.semaphore_signal(barrier, inc=1, device_id=other(k), device_id_type=MESH)

    def exchange(stage, c, send, recv):
        @pl.loop(0, grid - 1)
        def _(j):
            k = grid // 2 + ((j + 1) // 2) * (2 * lax.rem(j + 1, 2) - 1)
            peer = lax.rem(me + k, grid)
            pltpu.make_async_remote_copy(
                src_ref=send.at[c, :, peer],
                dst_ref=recv.at[c, :, me],
                send_sem=send_sems.at[stage, c],
                recv_sem=recv_sems.at[stage, c],
                device_id={"grid": peer},
                device_id_type=MESH,
            ).start()

        for s in range(subs):
            recv[c, s, me] = send[c, s, me]

    def arrived(stage, c, recv):
        part = recv.at[c, :, pl.ds(0, grid - 1)]
        pltpu.make_async_copy(part, part, recv_sems.at[stage, c]).wait()

    def sent(stage, c, send):
        part = send.at[c, :, pl.ds(0, grid - 1)]
        pltpu.make_async_copy(part, part, send_sems.at[stage, c]).wait()

    def doubled(rows, inner):
        mode = lax.rem(lax.broadcasted_iota(jnp.int32, (rows, 1), 0) // inner, sz.own)
        return jnp.where(mode + me * sz.own == 0, 1.0, 2.0).astype(F32)

    def row_tile(t):
        return pl.ds(pl.multiple_of(t * TILE, TILE), TILE)

    def mix_tile(j, t):
        return pl.ds(pl.multiple_of(j * sz.modes + t * TILE, TILE), TILE)

    def lanes(j):
        return pl.ds(128 * j, 128)

    def wide(j):
        return pl.ds(256 * j, 256)

    def send_columns(c, table, send):
        for s in range(subs):
            cells = pl.ds(s * sz.sub_cells, sz.sub_cells)
            high = hi_v[cells, :]
            out = dot(table[0], high) + dot(table[0], lo_v[cells, :]) + dot(table[1], high)
            send[c, s] = out.astype(BF16).reshape(grid, 16, feats)

    def both_parts(ref, j):
        return jnp.concatenate([ref[0, :, lanes(j)], ref[1, :, lanes(j)]], axis=1)

    def bias_parts(ref, j):
        return jnp.concatenate([ref[0:1, lanes(j)], ref[1:2, lanes(j)]], axis=1)

    @pl.loop(0, chunks)
    def _(c):
        pltpu.make_async_copy(x_hbm.at[c], x_v.at[c], sem_x.at[c]).wait()

        @each_tile(CELLS)
        def _(t):
            xhat, scale = moments(x_v[c, row_tile(t), :].astype(F32))
            hi_v[row_tile(t), :], lo_v[row_tile(t), :] = split(xhat * gain1[...] + bias1[...])

        send_columns(c, t_f, send_a)

        @pl.when(c == 0)
        def _():
            pl.semaphore_wait(barrier, everyone - 1)

        exchange(0, c, send_a, recv_a)


    pick_row = lax.broadcasted_iota(jnp.int32, (BSIZE, 128), 0)
    pick_lane = lax.broadcasted_iota(jnp.int32, (BSIZE, 128), 1)
    picks = [(pick_lane == pick_row + BSIZE * side).astype(F32).astype(BF16) for side in range(2)]
    for raw, big in ((sw1, w1), (sw2, w2)):
        for j in range(groups):
            real, imag = [
                jnp.concatenate([dot(raw[r, 2 * j + side], picks[side]) for side in range(2)], axis=0) for r in range(2)
            ]
            big[j, :128, :128] = real.astype(BF16)
            big[j, :128, 128:] = imag.astype(BF16)
            big[j, 128:, :128] = (-imag).astype(BF16)
            big[j, 128:, 128:] = real.astype(BF16)

    width = feats // masks.shape[0]

    @pl.loop(0, sz.items)
    def _(i):
        kind = ids[i]
        for g in range(masks.shape[0]):
            live[i, :, pl.ds(g * width, width)] = jnp.full((1, width), masks[g, kind].astype(F32))
        weight[i] = jnp.full((1, feats), counts[kind].astype(F32) * 0.125)

    for s in range(dm_acc.shape[0]):

        def clear(o, n):
            dm_acc[s, pl.ds(o, n), :] = jnp.zeros((n, feats), F32)

        tiled(dm_acc.shape[1], clear)
    dw1[...] = jnp.zeros_like(dw1)
    dw2[...] = jnp.zeros_like(dw2)
    dvec[...] = jnp.zeros_like(dvec)
    sums[...] = jnp.zeros_like(sums)

    @pl.loop(0, chunks)
    def _(c):
        arrived(0, c, recv_a)
        for s in range(subs):
            got = recv_a[c, s].reshape(grid * 16, feats)
            out = (dot(t_rf[0], got) + dot(t_rf[1], got)).astype(BF16)
            at = pl.ds(s * sz.sub_modes, sz.sub_modes)
            spec[c, 0, at, :] = out[: sz.sub_modes]
            spec[c, 1, at, :] = out[sz.sub_modes :]
        for j in range(groups):
            pul_s[pl.ds(j * sz.modes, sz.modes), :256] = dot(both_parts(spec.at[c], j), w1[j])
        for j in range(groups):

            @each_tile(sz.modes)
            def _(t):
                at = row_tile(t)
                act, slope = gelu_parts(pul_s[mix_tile(j, t), :256] + bias_parts(sb1, j))
                act1[c, at, wide(j)] = act.astype(BF16)
                slope1[c, at, wide(j)] = slope

        for j in range(groups):
            pul_s[pl.ds(j * sz.modes, sz.modes), :256] = dot(act1[c, :, wide(j)], w2[j])
        for j in range(groups):

            @each_tile(sz.modes)
            def _(t):
                at = row_tile(t)
                mixed = pul_s[mix_tile(j, t), :256] + bias_parts(sb2, j)
                bend = jnp.tanh(mixed * (1.0 / SHRINK))
                slope2[c, at, wide(j)] = bend * bend
                shrunk = (mixed - SHRINK * bend).astype(BF16)
                gbt[mix_tile(0, t), lanes(j)] = shrunk[:, :128]
                gbt[mix_tile(1, t), lanes(j)] = shrunk[:, 128:]

        for s in range(subs):
            at = pl.ds(s * sz.sub_modes, sz.sub_modes)
            second, third, fourth = [pl.ds(k * modes + s * sz.sub_modes, sz.sub_modes) for k in (1, 2, 3)]
            high = jnp.concatenate([gbt[at, :], gbt[second, :]], axis=0)
            out = (dot(t_rb[0], high) + dot(t_rb[1], high)) * doubled(grid * 16, 2)
            send_b[c, s] = out.astype(BF16).reshape(grid, 16, feats)
        exchange(1, c, send_b, recv_b)

    load_win.wait()
    load_wout.wait()

    def feed_forward(c):
        pltpu.make_async_copy(cot_hbm.at[c], cot_v.at[c], sem_cot.at[c]).wait()
        arrived(1, c, recv_b)
        for s in range(subs):
            cells = pl.ds(s * sz.sub_cells, sz.sub_cells)
            got = recv_b[c, s].reshape(grid * 16, feats)
            gres[c, cells, :] = dot(t_b[0], got) + dot(t_b[1], got)

        @each_tile(CELLS)
        def _(t):
            at = row_tile(t)
            item = c * sz.chunk_items + (t * TILE) // sz.item_cells
            total = x_v[c, at, :].astype(F32) + live[item] * gres[c, at, :]
            gres[c, at, :] = total
            xhat, scale = moments(total)
            n2[at, :] = (xhat * gain2[...] + bias2[...]).astype(BF16)
            grad = (cot_v[c, at, :].astype(F32) * weight[item]).astype(BF16)
            gb[at, :] = grad
            sums[BOUT] += eight_rows(grad.astype(F32))

        n2t[...] = n2[...].T
        gbt[...] = gb[...].T

        def products(f):
            at = pl.ds(f * FT, FT)
            hid_s[...] = dot(n2[...], w_in[:, at])
            pul_s[...] = dot_nt(gb[...], w_out[at, :])

        for f in range(blocks):
            products(f)
            at = pl.ds(f * FT, FT)

            @each_tile(CELLS)
            def _(t):
                rows = row_tile(t)
                act, slope = gelu_parts(hid_s[rows, :] + b_in[:, at])
                act_s[rows, at] = act.astype(BF16)
                grad = (slope * pul_s[rows, :]).astype(BF16)
                gh_s[rows, at] = grad
                sums[BIN + f] += eight_rows(grad.astype(F32))

        hid_s[...] = dot_nt(gh_s[...], w_in[...])
        pul_s[...] = dot(act_s[...], w_out[...])

        @each_tile(CELLS)
        def _(t):
            at = row_tile(t)
            item = c * sz.chunk_items + (t * TILE) // sz.item_cells
            total = gres[c, at, :]
            xhat, scale = moments(total)
            grad = hid_s[at, :]
            sums[GAIN2] += eight_rows(grad * xhat)
            sums[BIAS2] += eight_rows(grad)
            grad_out = cot_v[c, at, :].astype(F32) * weight[item]
            cot_v[c, at, :] = (total + pul_s[at, :] + b_out[...]).astype(BF16)
            out = grad_out + pull_norm(grad, xhat, scale, gain2[...])
            gres[c, at, :] = out
            hi_v[at, :], lo_v[at, :] = split(out * live[item])

        sent(0, c, send_a)
        send_columns(c, t_f, send_a)
        exchange(2, c, send_a, recv_a)
        pltpu.make_async_copy(cot_v.at[c], act_hbm.at[c], sem_out.at[c]).start()
        for f in range(blocks):
            at, into = pl.ds(f * FT, FT), pl.ds((f % 2) * feats, feats)
            dm_acc[f // 2, into, :] += dot(n2t[...], gh_s[:, at])
            dm_acc[blocks // 2 + f // 2, into, :] += dot(gbt[...], act_s[:, at])

    def dz_of(j):
        return n2t[pl.ds((j // 2) * modes, modes), wide(j % 2)]

    def dm_of(j):
        return n2t[pl.ds((2 + j // 2) * modes, modes), wide(j % 2)]

    def mix_backward(c):
        arrived(2, c, recv_a)
        for s in range(subs):
            got = recv_a[c, s].reshape(grid * 16, feats)
            out = (dot(t_rf[0], got) + dot(t_rf[1], got)) * doubled(2 * sz.sub_modes, MODES)
            at = pl.ds(s * sz.sub_modes, sz.sub_modes)
            hid_s[at, :] = out[: sz.sub_modes]
            hid_s[pl.ds(sz.modes + s * sz.sub_modes, sz.sub_modes), :] = out[sz.sub_modes :]
        for j in range(groups):

            @each_tile(sz.modes)
            def _(t):
                at = row_tile(t)
                low_at = pl.ds(pl.multiple_of(sz.modes + t * TILE, TILE), TILE)
                both = jnp.concatenate([hid_s[at, lanes(j)], hid_s[low_at, lanes(j)]], axis=1)
                dz = (both * slope2[c, at, wide(j)]).astype(BF16)
                n2t[mix_tile(j // 2, t), wide(j % 2)] = dz
                dz = eight_rows(dz.astype(F32))
                for r in range(2):
                    sums[SB2 + r, :, lanes(j)] += dz[:, 128 * r : 128 * r + 128]

        for j in range(groups):
            pul_s[pl.ds(j * sz.modes, sz.modes), :256] = dot_nt(dz_of(j), w2[j])
        for j in range(groups):

            @each_tile(sz.modes)
            def _(t):
                at = row_tile(t)
                dm = (pul_s[mix_tile(j, t), :256] * slope1[c, at, wide(j)]).astype(BF16)
                n2t[mix_tile(2 + j // 2, t), wide(j % 2)] = dm
                dm = eight_rows(dm.astype(F32))
                for r in range(2):
                    sums[SB1 + r, :, lanes(j)] += dm[:, 128 * r : 128 * r + 128]

        for j in range(groups):
            pul_s[pl.ds(j * sz.modes, sz.modes), :256] = dot_nt(dm_of(j), w1[j])
        for j in range(groups):

            @each_tile(sz.modes)
            def _(t):
                at = row_tile(t)
                high, low = split(pul_s[mix_tile(j, t), :256])
                for r in range(2):
                    gbt[mix_tile(r, t), lanes(j)] = high[:, 128 * r : 128 * r + 128]
                    gbt[mix_tile(2 + r, t), lanes(j)] = low[:, 128 * r : 128 * r + 128]

        sent(1, c, send_b)
        for s in range(subs):
            at = pl.ds(s * sz.sub_modes, sz.sub_modes)
            second, third, fourth = [pl.ds(k * modes + s * sz.sub_modes, sz.sub_modes) for k in (1, 2, 3)]
            high = jnp.concatenate([gbt[at, :], gbt[second, :]], axis=0)
            low = jnp.concatenate([gbt[third, :], gbt[fourth, :]], axis=0)
            out = dot(t_rb[0], high) + dot(t_rb[0], low) + dot(t_rb[1], high)
            send_b[c, s] = out.astype(BF16).reshape(grid, 16, feats)
        exchange(3, c, send_b, recv_b)
        for j in range(groups):
            dz, dm = dz_of(j), dm_of(j)
            dw2[j] += dot_tn(act1[c, :, wide(j)], dz)
            dw1[j] += dot_tn(both_parts(spec.at[c], j), dm)

    def near_of(s, off, size):
        return w_in.at[pl.ds(pl.multiple_of(off, 16), size), pl.ds(s * FT, FT)]

    def near_mixing(off, size):
        return ds_near.at[pl.ds(pl.multiple_of(off, 16), size)]

    segments = [
        Reducer(
            dm_acc.at[s], (act_s.at[:, pl.ds(s * FT, FT)], gh_s.at[:, pl.ds(s * FT, FT)]), dm_land.at[s], functools.partial(near_of, s),
            dm_send.at[s], dm_recv.at[s], order if s < blocks // 2 else swapped, index,
        )
        for s in range(blocks)
    ]

    def all_of(group, k):
        for one in group:
            one.ticks()[k]()

    mix_piece, vec_piece = mix_rows // (2 * grid), 16 * groups // (2 * grid)
    half_side = lax.rem(index["batch"], 2)

    def partner(bit):
        side = lax.rem(index["batch"] // 2**bit, 2)
        return {"batch": index["batch"] + (1 - 2 * side) * 2**bit}

    def late_copy(step, source, target, device):
        return pltpu.make_async_remote_copy(
            src_ref=source, dst_ref=target, send_sem=late_send.at[step], recv_sem=late_recv.at[step],
            device_id=device, device_id_type=MESH,
        )

    def late_halves(bit):
        return late_copy(bit, late_stage.at[bit], late_land.at[bit], partner(bit))

    def late_pieces(step, k):
        peer = lax.rem(me + k, grid)
        if step == batch_bits:
            return late_copy(step, late_split.at[peer], late_parts.at[me], {"grid": peer})
        return late_copy(step, late_near.at[me], late_near.at[me], {"grid": peer})

    def late_home():
        return late_copy(batch_bits + 2, late_near, late_far, partner(0))

    def late_first():
        late_acc[...] = jnp.zeros_like(late_acc)
        for layer, big in enumerate((dw1, dw2)):
            for j in range(groups):
                real = big[j, :128, :128] + big[j, 128:, 128:]
                imag = big[j, :128, 128:] - big[j, 128:, :128]
                for r, part in enumerate((real, imag)):
                    part = jnp.where(pick_lane < BSIZE, part[:BSIZE], part[BSIZE:])
                    for o in range(0, BSIZE, mix_piece):
                        row = ((layer * 2 + r) * groups + j) * BSIZE + o
                        n = min(mix_piece, BSIZE)
                        piece, into = row // mix_piece, row % mix_piece
                        late_acc[piece // grid, piece % grid, into : into + n, :] = part[o : o + n]
        for row in range(SB1, 16):
            dvec[row : row + 1, :] = jnp.sum(sums[row], axis=0, keepdims=True)
        vectors = jnp.concatenate([dvec[:, lanes(j)] for j in range(groups)], axis=0)
        for piece in range(2 * grid):
            late_acc[piece // grid, piece % grid, mix_piece : mix_piece + vec_piece, :] = vectors[
                piece * vec_piece : (piece + 1) * vec_piece
            ]
        late_stage[0] = late_acc[1 - half_side].astype(BF16)
        late_halves(0).start()

    def late_second():
        late_halves(0).wait_recv()
        total = late_acc[half_side] + late_land[0].astype(F32)
        for bit in range(1, batch_bits):
            late_stage[bit] = total.astype(BF16)
            late_halves(bit).start()
            late_halves(bit).wait_recv()
            total = late_stage[bit].astype(F32) + late_land[bit].astype(F32)
        late_split[...] = total.astype(BF16)

        @pl.loop(1, grid)
        def _(k):
            late_pieces(batch_bits, k).start()

    def late_wait(ref, step):
        part = ref.at[pl.ds(0, grid - 1)]
        pltpu.make_async_copy(part, part, late_recv.at[step]).wait()

    def late_third():
        late_wait(late_parts, batch_bits)
        late_parts[me] = late_split[me]
        total = late_parts[0].astype(F32)
        for g in range(1, grid):
            total = total + late_parts[g].astype(F32)
        late_near[me] = total.astype(BF16)

        @pl.loop(1, grid)
        def _(k):
            late_pieces(batch_bits + 1, k).start()

    def late_fourth():
        late_wait(late_near, batch_bits + 1)
        late_home().start()

    def late_fifth():
        late_home().wait_recv()

    def late_sent():
        for bit in range(batch_bits):
            late_halves(bit).wait_send()

        @pl.loop(1, grid)
        def _(k):
            late_pieces(batch_bits, k).wait_send()
            late_pieces(batch_bits + 1, k).wait_send()

        late_home().wait_send()

    queues = {
        "e": [functools.partial(all_of, segments[0::2], k) for k in range(len(segments[0].ticks()))],
        "f": [functools.partial(all_of, segments[1::2], k) for k in range(len(segments[0].ticks()))],
        "l": [late_first, late_second, late_third, late_fourth, late_fifth],
    }

    def run(names):
        for name in names:
            if queues[name]:
                queues[name].pop(0)()

    def finish_inputs(c):
        arrived(3, c, recv_b)
        for s in range(subs):
            cells = pl.ds(s * sz.sub_cells, sz.sub_cells)
            got = recv_b[c, s].reshape(grid * 16, feats)
            hid_s[cells, :] = dot(t_b[0], got) + dot(t_b[1], got)

        @each_tile(CELLS)
        def _(t):
            at = row_tile(t)
            xhat, scale = moments(x_v[c, at, :].astype(F32))
            grad = hid_s[at, :]
            sums[GAIN1] += eight_rows(grad * xhat)
            sums[BIAS1] += eight_rows(grad)
            gres[c, at, :] += pull_norm(grad, xhat, scale, gain1[...])

        pltpu.make_async_copy(gres.at[c], ig_hbm.at[c], sem_ig.at[c]).start()

    @pl.loop(0, 2 * chunks)
    def _(c):
        @pl.when(c < chunks)
        def _():
            feed_forward(c)

        @pl.when(c == chunks - 1)
        def _():
            run("ef")

        @pl.when(jnp.logical_and(c >= 2, c < chunks + 2))
        def _():
            mix_backward(c - 2)

        @pl.when(c == chunks - 1)
        def _():
            run("e")

        @pl.when(c == chunks)
        def _():
            run("fe")

        @pl.when(c == chunks + 1)
        def _():
            run("l")

        @pl.when(c >= chunks)
        def _():
            finish_inputs(c - chunks)

        for k, names in enumerate(("fe", "felfe", "felfelfel")[: chunks - 1]):

            @pl.when(c == chunks + k)
            def _():
                run(names)

    last = [jnp.sum(sums[row], axis=0, keepdims=True) for row in (GAIN1, BIAS1)]
    own = jnp.concatenate([last[k % 2][:, 128 * (k // 2) : 128 * (k // 2) + 128] for k in range(2 * groups)], axis=0)
    n1_send[...] = own
    n1_recv[my_place] = own

    def n1_copy(k):
        return pltpu.make_async_remote_copy(
            src_ref=n1_send, dst_ref=n1_recv.at[my_place], send_sem=n1_ssem, recv_sem=n1_rsem,
            device_id=other(k), device_id_type=MESH,
        )

    @pl.loop(1, everyone)
    def _(k):
        n1_copy(k).start()

    while any(queues.values()):
        run("lef")
    for side, held in enumerate((late_near, late_far)):
        place = half_side if side == 0 else 1 - half_side
        dspec_out[place] = held[:, :mix_piece, :].reshape(mix_rows // 2, 128)
        for g in range(grid):
            late_acc[place, g, mix_piece : mix_piece + vec_piece, :] = held[
                g, mix_piece : mix_piece + vec_piece, :
            ].astype(F32)
    for piece in range(2 * grid):
        for k in range(vec_piece):
            row = piece * vec_piece + k
            dvec_out[row % 16, lanes(row // 16)] = late_acc[piece // grid, piece % grid, mix_piece + k, :]
    part = n1_recv.at[pl.ds(0, everyone - 1)]
    pltpu.make_async_copy(part, part, n1_rsem).wait()
    total = n1_recv[0]
    for g in range(1, everyone):
        total = total + n1_recv[g]
    for j in range(groups):
        dvec_out[0:2, lanes(j)] = total[2 * j : 2 * j + 2, :]

    outs = []
    halves_of = blocks // 2
    for half, turned in zip(range(halves_of), (n2, n2t)):
        near_in, near_out = [pl.ds((half + m * halves_of) * FT, FT) for m in range(2)]
        outs.append(pltpu.make_async_copy(w_in.at[:, near_in], near_hbm.at[half], sem_dm.at[half]))
        outs[-1].start()
        turned[...] = w_in[:, near_out].T
        outs.append(pltpu.make_async_copy(turned, near_hbm.at[halves_of + half], sem_dm.at[halves_of + half]))
        outs[-1].start()

    for one in segments:
        one.wait_sent()
    late_sent()

    @pl.loop(1, everyone)
    def _(k):
        n1_copy(k).wait_send()

    @pl.loop(0, chunks)
    def _(c):
        sent(2, c, send_a)
        sent(3, c, send_b)
        pltpu.make_async_copy(cot_v.at[c], act_hbm.at[c], sem_out.at[c]).wait()
        pltpu.make_async_copy(gres.at[c], ig_hbm.at[c], sem_ig.at[c]).wait()

    for copy in outs:
        copy.wait()


def finish(
    sz,
    act_in, ig_in, near_in, dspec, dvec,
    act_hbm, ig_hbm, gain1, bias1, sw1, sb1, sw2, sb2, gain2, bias2, dmi_hbm, b_in, dmo_hbm, b_out,
    act_v, ig_v, near_v, near_f, sem_in, sem_out,
):
    chunks, feats, hidden = sz.chunks, sz.feats, sz.hidden
    widened = widen(near_in, near_v, near_f, dmi_hbm, dmo_hbm, lax.rem(lax.axis_index("batch"), 2), sem_in, sem_out)
    moves = []
    for c in range(chunks):
        for m, (source, held, target) in enumerate(((ig_in, ig_v, ig_hbm), (act_in, act_v, act_hbm))):
            k = 2 * near_v.shape[0] + 2 * c + m
            moves.append(
                (
                    pltpu.make_async_copy(source.at[c], held.at[c], sem_in.at[k]),
                    pltpu.make_async_copy(held.at[c], target.at[c], sem_out.at[k]),
                )
            )
    next(widened)
    for fetch, store in moves:
        fetch.start()
    for layer, out in enumerate((sw1, sw2)):
        for side in range(2):
            row = lax.broadcasted_iota(jnp.int32, (128, BSIZE), 0)
            lane = lax.broadcasted_iota(jnp.int32, (128, BSIZE), 1)
            pick = (row == lane + BSIZE * side).astype(F32).astype(BF16)
            picked = dot(dspec[layer], pick)
            for r in range(2):
                for j in range(BLOCKS // 2):
                    at = (r * (BLOCKS // 2) + j) * BSIZE
                    out[r, 2 * j + side] = picked[at : at + BSIZE]
    for row, out in ((GAIN1, gain1), (BIAS1, bias1), (GAIN2, gain2), (BIAS2, bias2), (BOUT, b_out)):
        out[...] = dvec[row : row + 1, :]
    sb1[...] = dvec[SB1 : SB1 + 2, :]
    sb2[...] = dvec[SB2 : SB2 + 2, :]
    for f in range(hidden // feats):
        b_in[:, f * feats : (f + 1) * feats] = dvec[BIN + f : BIN + f + 1, :]
    next(widened)
    for fetch, store in moves:
        fetch.wait()
        store.start()
    for fetch, store in moves:
        store.wait()
    for _ in widened:
        pass


def widen(source, held, wide, dmi_hbm, dmo_hbm, side, sem_in, sem_out):
    halves_of, feats = source.shape[0] // 2, source.shape[1]
    rows = feats // 2
    moves = []
    for block in range(2 * halves_of):
        at = pl.ds(pl.multiple_of((2 * (block % halves_of) + side) * FT, FT), FT)
        for part in range(2):
            here = pl.ds(part * rows, rows)
            if block < halves_of:
                target = dmi_hbm.at[here, at]
            else:
                target = dmo_hbm.at[pl.ds(pl.multiple_of((2 * (block % halves_of) + side) * FT + part * rows, rows), rows)]
            k = 2 * block + part
            moves.append(
                (
                    pltpu.make_async_copy(source.at[block, here], held.at[block, here], sem_in.at[k]),
                    pltpu.make_async_copy(wide.at[block, here], target, sem_out.at[k]), block, here,
                )
            )
    for fetch, store, block, here in moves:
        fetch.start()
    yield
    for fetch, store, block, here in moves:
        fetch.wait()
        for o in range(0, rows, COPY):
            at = pl.ds(here.start + o, COPY)
            wide[block, at, :] = held[block, at, :].astype(F32)
        store.start()
    yield
    for fetch, store, block, here in moves:
        store.wait()


def finish_far(far_in, dmi_in, dmo_in, dmi_hbm, dmo_hbm, far_v, far_f, sem_in, sem_out):
    side = 1 - lax.rem(lax.axis_index("batch"), 2)
    for _ in widen(far_in, far_v, far_f, dmi_hbm, dmo_hbm, side, sem_in, sem_out):
        pass


def local(
    batch, grid,
    inputs, cotangent, dataset_ids, channel_masks, sample_counts, norm1_gain, norm1_bias,
    spec_w1, spec_b1, spec_w2, spec_b2, norm2_gain, norm2_bias, mlp_in, mlp_in_bias, mlp_out, mlp_out_bias,
):
    items, rows, cols, feats = inputs.shape
    hidden = mlp_in.shape[1]
    sz = sizes_of(items, rows, cols, feats, hidden, grid)
    batch_bits, grid_bits = batch.bit_length() - 1, grid.bit_length() - 1
    bits = batch_bits + grid_bits

    vmem = pl.BlockSpec(memory_space=pltpu.VMEM)
    smem = pl.BlockSpec(memory_space=pltpu.SMEM)
    hbm = pl.BlockSpec(memory_space=pl.ANY)
    chunks, groups, blocks = sz.chunks, feats // 128, hidden // FT
    shape = (chunks, CELLS, feats)
    pieces = (chunks, sz.subs, grid, 16, feats)
    seg_rows = 2 * feats
    mix_rows = 4 * groups * BSIZE
    late = (grid, mix_rows // (2 * grid) + 16, 128)
    out_shape = (
        jax.ShapeDtypeStruct(shape, BF16),
        jax.ShapeDtypeStruct(shape, F32),
        jax.ShapeDtypeStruct((blocks, feats, FT), BF16),
        jax.ShapeDtypeStruct((2, mix_rows // 2, 128), BF16),
        jax.ShapeDtypeStruct((16, feats), F32),
    )
    dma = pltpu.SemaphoreType.DMA
    scratch = [
        pltpu.VMEM(shape, BF16),
        pltpu.VMEM(shape, BF16),
        pltpu.VMEM(mlp_in.shape, BF16),
        pltpu.VMEM(mlp_out.shape, BF16),
        *[pltpu.VMEM(pieces, BF16)] * 4,
        pltpu.VMEM(shape, F32),
        pltpu.VMEM((chunks, 2, sz.modes, feats), BF16),
        pltpu.VMEM((chunks, sz.modes, 2 * feats), BF16),
        pltpu.VMEM((chunks, sz.modes, 2 * feats), F32),
        pltpu.VMEM((chunks, sz.modes, 2 * feats), F32),
        pltpu.VMEM((groups, 256, 256), BF16),
        pltpu.VMEM((groups, 256, 256), BF16),
        pltpu.VMEM((groups, 256, 256), F32),
        pltpu.VMEM((groups, 256, 256), F32),
        pltpu.VMEM((CELLS, feats), BF16),
        pltpu.VMEM((feats, CELLS), BF16),
        pltpu.VMEM((CELLS, feats), BF16),
        pltpu.VMEM((feats, CELLS), BF16),
        pltpu.VMEM((CELLS, hidden), BF16),
        pltpu.VMEM((CELLS, hidden), BF16),
        pltpu.VMEM((items, 1, feats), F32),
        pltpu.VMEM((items, 1, feats), F32),
        pltpu.VMEM((blocks, seg_rows, FT), F32),
        pltpu.VMEM((blocks, landing_rows(seg_rows, bits), FT), BF16),
        pltpu.VMEM((2, *late), F32),
        pltpu.VMEM((batch_bits, *late), BF16),
        pltpu.VMEM((batch_bits, *late), BF16),
        *[pltpu.VMEM(late, BF16)] * 4,
        pltpu.VMEM((16, feats), F32),
        pltpu.VMEM((16, 8, feats), F32),
        pltpu.VMEM((CELLS, FT), F32),
        pltpu.VMEM((CELLS, FT), F32),
        pltpu.VMEM((2 * groups, 128), F32),
        pltpu.VMEM((batch * grid, 2 * groups, 128), F32),
        dma((chunks,)),
        dma((chunks,)),
        dma((2,)),
        dma((chunks,)),
        dma((chunks,)),
        dma((blocks,)),
        *[dma((4, chunks))] * 2,
        dma((blocks, 2 * bits)),
        dma((blocks, 2 * bits)),
        dma((batch_bits + 3,)),
        dma((batch_bits + 3,)),
        dma,
        dma,
    ]
    cells = items * rows * cols
    row = lambda v: v.reshape(1, -1)
    parts = pl.pallas_call(
        functools.partial(kernel, sz, batch_bits, grid_bits),
        out_shape=out_shape,
        in_specs=[smem] * 3 + [hbm, hbm] + [vmem] * 14 + [hbm, hbm],
        out_specs=(hbm, hbm, hbm, vmem, vmem),
        scratch_shapes=scratch,
        cost_estimate=pl.CostEstimate(
            flops=14 * cells * feats * hidden, bytes_accessed=24 << 20, transcendentals=3 * cells * hidden
        ),
        compiler_params=pltpu.CompilerParams(
            collective_id=0, has_side_effects=True, vmem_limit_bytes=67_000_000
        ),
    )(
        dataset_ids, channel_masks.T, sample_counts,
        inputs.reshape(shape), cotangent.reshape(shape),
        row(norm1_gain), row(norm1_bias), row(norm2_gain), row(norm2_bias),
        spec_w1, spec_b1, spec_w2, spec_b2, row(mlp_in_bias), row(mlp_out_bias),
        *[jnp.asarray(t) for t in tables(sz)], mlp_in, mlp_out,
    )
    vector = jax.ShapeDtypeStruct((1, feats), F32)
    pair = jax.ShapeDtypeStruct((2, feats), F32)
    mixers = jax.ShapeDtypeStruct(spec_w1.shape, F32)
    moves = 2 * blocks + 2 * chunks
    half_shape = (blocks, feats, FT)
    outs = pl.pallas_call(
        functools.partial(finish, sz),
        out_shape=(
            out_shape[0], out_shape[1], vector, vector, mixers, pair, mixers, pair, vector, vector,
            jax.ShapeDtypeStruct(mlp_in.shape, F32), jax.ShapeDtypeStruct((1, hidden), F32),
            jax.ShapeDtypeStruct(mlp_out.shape, F32), vector,
        ),
        in_specs=[hbm] * 3 + [vmem] * 2,
        out_specs=(hbm, hbm) + (vmem,) * 8 + (hbm, vmem, hbm, vmem),
        scratch_shapes=[
            pltpu.VMEM(shape, BF16), pltpu.VMEM(shape, F32), pltpu.VMEM(half_shape, BF16), pltpu.VMEM(half_shape, F32),
            dma((moves,)), dma((moves,)),
        ],
        cost_estimate=pl.CostEstimate(flops=0, bytes_accessed=24 << 20, transcendentals=0),
        compiler_params=pltpu.CompilerParams(vmem_limit_bytes=67_000_000),
    )(*parts)
    far = lax.ppermute(parts[2], "batch", [(b, b ^ 1) for b in range(batch)])
    wide = (jax.ShapeDtypeStruct(mlp_in.shape, F32), jax.ShapeDtypeStruct(mlp_out.shape, F32))
    dmi, dmo = pl.pallas_call(
        finish_far,
        out_shape=wide,
        in_specs=[hbm] * 3,
        out_specs=(hbm, hbm),
        input_output_aliases={1: 0, 2: 1},
        scratch_shapes=[
            pltpu.VMEM(half_shape, BF16), pltpu.VMEM(half_shape, F32), dma((2 * blocks,)), dma((2 * blocks,)),
        ],
        cost_estimate=pl.CostEstimate(flops=0, bytes_accessed=6 << 20, transcendentals=0),
        compiler_params=pltpu.CompilerParams(vmem_limit_bytes=67_000_000),
    )(far, outs[10], outs[12])
    flat = lambda v: v.reshape(-1)
    return (
        outs[0].reshape(inputs.shape), outs[1].reshape(inputs.shape), flat(outs[2]), flat(outs[3]), *outs[4:8],
        flat(outs[8]), flat(outs[9]), dmi, flat(outs[11]), dmo, flat(outs[13]),
    )


def solution(mesh):
    spread = P("batch", "grid", None, None)
    return jax.shard_map(
        functools.partial(local, mesh.shape["batch"], mesh.shape["grid"]),
        mesh=mesh,
        in_specs=(spread, spread, P("batch")) + (P(),) * 14,
        out_specs=(spread, spread) + (P(),) * 12,
        check_vma=False,
    )
```

```python
import functools
import math

import jax
import jax.numpy as jnp
import numpy as np
from jax import lax
from jax.experimental import pallas as pl
from jax.experimental.pallas import tpu as pltpu
from jax.sharding import PartitionSpec as P

BLOCKS = 8
MODES = 32
BSIZE = 64
EPSILON = 1e-06
SHRINK = 0.1
MESH = pl.DeviceIdType.MESH
F32 = jnp.float32
BF16 = jnp.bfloat16
CELLS = 512
TILE = 16
COPY = 32
FT = 512


def sizes_of(items, rows, cols, feats, hidden, grid):
    sz = type("Sizes", (), {})()
    sz.items, sz.rows, sz.cols, sz.feats, sz.hidden, sz.grid = items, rows, cols, feats, hidden, grid
    sz.own = MODES // grid
    sz.plane = math.gcd(grid, 4)
    sz.planes = grid // sz.plane
    sz.height = rows * grid
    sz.item_cells = rows * cols
    sz.sub_items = 16 // (rows * sz.own * 2)
    sz.sub_cells = sz.sub_items * sz.item_cells
    sz.subs = CELLS // sz.sub_cells
    sz.chunk_items = sz.subs * sz.sub_items
    sz.chunks = items // sz.chunk_items
    sz.sub_modes = sz.sub_items * sz.own * MODES
    sz.modes = sz.subs * sz.sub_modes
    return sz


def halves(table):
    high = table.astype(BF16)
    low = (table - high.astype(np.float64)).astype(BF16)
    return np.stack([high, low])


def tables(sz):
    its, rows, own, cols, grid = sz.sub_items, sz.rows, sz.own, sz.cols, sz.grid
    w = np.arange(cols)
    q = np.arange(MODES)
    angle = 2 * np.pi * (np.outer(q, w) % cols) / cols
    col = np.stack([np.cos(angle), -np.sin(angle)], axis=1) / math.sqrt(cols)
    lines = its * rows
    eye = np.eye(lines)

    def placed(tab):
        tab = tab.reshape(grid, own, 2, cols)
        big = np.einsum("gqrw,lm->glqrmw", tab, eye)
        return big.reshape(grid * 16, lines * cols)

    first = placed(col)
    p = np.where(q < MODES // 2, q, sz.height - MODES + q)
    h = np.arange(sz.height)
    angle = 2 * np.pi * (np.outer(p, h) % sz.height) / sz.height
    cosine, sine = np.cos(angle), np.sin(angle)
    row = np.stack([np.stack([cosine, sine], -1), np.stack([-sine, cosine], -1)], 1) / math.sqrt(sz.height)
    row = row.reshape(MODES, 2, grid, rows, 2)
    big = np.einsum("psghr,ij,qk->siqpgjhkr", row, np.eye(its), np.eye(own))
    big = big.reshape(2 * sz.sub_modes, grid * 16)
    return [halves(t) for t in (first, first.T, big, big.T)]


def dot(a, b):
    return jnp.dot(a, b, preferred_element_type=F32)


def dot_nt(a, b):
    return lax.dot_general(a, b, (((1,), (1,)), ((), ())), preferred_element_type=F32)


def dot_tn(a, b):
    return lax.dot_general(a, b, (((0,), (0,)), ((), ())), preferred_element_type=F32)


def split(v):
    high = v.astype(BF16)
    return high, (v - high.astype(F32)).astype(BF16)


CDF = (
    0.797884941492634, 0.03633308439449127, -3.259472654998994e-05, -5.530632529808752e-05, 3.964774886835927e-06,
    -1.3226642974616402e-07, 1.756281964154736e-09,
)


def gelu_parts(v):
    square = v * v
    inner = jnp.minimum(square, 30.0)
    q = CDF[6] * inner + CDF[5]
    for coef in CDF[4::-1]:
        q = q * inner + coef
    cdf = 0.5 + 0.5 * jnp.tanh(v * q)
    pdf = jnp.exp2(square * (-0.5 * math.log2(math.e))) * (1.0 / math.sqrt(2.0 * math.pi))
    return v * cdf, cdf + v * pdf


def moments(v):
    centred = v - jnp.mean(v, axis=-1, keepdims=True)
    scale = lax.rsqrt(jnp.mean(centred * centred, axis=-1, keepdims=True) + EPSILON)
    return centred * scale, scale


def pull_norm(grad, xhat, scale, gain):
    gy = grad * gain
    return (gy - jnp.mean(gy, -1, keepdims=True) - xhat * jnp.mean(gy * xhat, -1, keepdims=True)) * scale


def eight_rows(v):
    return jnp.sum(v.reshape(v.shape[0] // 8, 8, v.shape[1]), axis=0)


GAIN1, BIAS1, SB1, SB2, GAIN2, BIAS2, BOUT, BIN = 0, 1, 2, 4, 6, 7, 8, 9


def tiled(count, body):
    size = min(count, COPY)

    @pl.loop(0, count // size, unroll=min(4, count // size))
    def _(t):
        body(t * size, size)


def each_tile(rows):
    return pl.loop(0, rows // TILE, unroll=rows // TILE)


def landing_rows(rows, bits):
    total = 0
    for _ in range(bits):
        rows = rows // 2 if rows % 32 == 0 else rows
        total += rows
    return total


class Pieces:
    def __init__(self, source, target, rows, send_sem, recv_sem, device):
        self.source, self.target, self.rows, self.device = source, target, rows, device
        self.send_sem, self.recv_sem = send_sem, recv_sem

    def part(self, at):
        return pltpu.make_async_remote_copy(
            src_ref=self.source.at[at], dst_ref=self.target.at[at], send_sem=self.send_sem, recv_sem=self.recv_sem,
            device_id=self.device, device_id_type=MESH,
        )

    def start(self):
        size = max(16, self.rows // 8)

        @pl.loop(0, self.rows // size)
        def _(k):
            self.part(pl.ds(pl.multiple_of(k * size, 16), size)).start()

    def wait_send(self):
        self.part(pl.ds(0, self.rows)).wait_send()

    def wait_recv(self):
        self.part(pl.ds(0, self.rows)).wait_recv()


class Reducer:
    def __init__(self, acc, stages, landing, near, send_sems, recv_sems, order, index):
        self.acc, self.stages, self.landing, self.near = acc, stages, landing, near
        self.send_sems, self.recv_sems = send_sems, recv_sems
        self.steps = []
        size, off, land = acc.shape[0], 0, 0
        for axis, bit in order:
            side = lax.rem(index[axis] // 2**bit, 2)
            partner = {axis: index[axis] + (1 - 2 * side) * 2**bit}
            halving = size % 32 == 0
            if halving:
                size = size // 2
                away, off = off + (1 - side) * size, off + side * size
            else:
                away = off
            self.steps.append((halving, size, away, off, land, partner))
            land += size
        self.off, self.size = off, size
        self.back = [k for k in reversed(range(1, len(order))) if self.steps[k][0]]

    def at(self, off, size):
        return pl.ds(pl.multiple_of(off, 16), size)

    def stage(self, k):
        halving, size, away, off, land, partner = self.steps[k]
        if not halving:
            return self.near(off - self.steps[0][3], size)
        return self.stages[0] if k == 0 else self.stages[1].at[pl.ds(land - self.steps[0][1], size)]

    def copy(self, k):
        halving, size, away, off, land, partner = self.steps[k]
        return Pieces(
            self.stage(k), self.landing.at[pl.ds(land, size)], size, self.send_sems.at[k], self.recv_sems.at[k], partner
        )

    def start(self, k):
        halving, size, away, off, land, partner = self.steps[k]

        stage = self.stage(k)

        def body(o, n):
            stage[pl.ds(o, n), :] = self.acc[self.at(away + o, n), :].astype(BF16)

        tiled(size, body)
        self.copy(k).start()

    def finish(self, k):
        halving, size, away, off, land, partner = self.steps[k]
        self.copy(k).wait_recv()
        if not halving:
            self.copy(k).wait_send()
        stage = self.stage(k)

        def body(o, n):
            at = self.at(off + o, n)
            mine = self.acc[at, :] if halving else stage[pl.ds(o, n), :].astype(F32)
            self.acc[at, :] = mine + self.landing[pl.ds(land + o, n), :].astype(F32)

        tiled(size, body)

    def begin_back(self):
        first = self.steps[0][3]

        def body(o, n):
            at = self.at(self.off + o, n)
            self.near(self.off - first + o, n)[...] = self.acc[at, :].astype(BF16)

        tiled(self.size, body)

    def back_copy(self, i):
        halving, size, away, off, land, partner = self.steps[self.back[i]]
        part = self.near(off - self.steps[0][3], size)
        sem = len(self.steps) + i
        return Pieces(part, part, size, self.send_sems.at[sem], self.recv_sems.at[sem], partner)

    def ticks(self):
        count, back = len(self.steps), len(self.back)

        def first():
            self.start(0)

        def forth(k):
            self.finish(k)
            if k + 1 < count:
                self.start(k + 1)
            else:
                self.begin_back()
                self.back_copy(0).start()

        def home(i):
            self.back_copy(i).wait_recv()
            if i + 1 < back:
                self.back_copy(i + 1).start()

        return (
            [first]
            + [functools.partial(forth, k) for k in range(count)]
            + [functools.partial(home, i) for i in range(back)]
        )

    def wait_sent(self):
        for k, step in enumerate(self.steps):
            if step[0]:
                self.copy(k).wait_send()
        for i in range(len(self.back)):
            self.back_copy(i).wait_send()


def kernel(
    sz, batch_bits, grid_bits,
    ids, masks, counts,
    x_hbm, cot_hbm, gain1, bias1, gain2, bias2, sw1, sb1, sw2, sb2, b_in, b_out,
    t_f, t_b, t_rf, t_rb, win_hbm, wout_hbm,
    act_hbm, ig_hbm, near_hbm, dspec_out, dvec_out,
    x_v, cot_v, w_in, w_out, send_a, recv_a, send_b, recv_b, gres,
    spec, act1, slope1, slope2, w1, w2, dw1, dw2,
    n2, n2t, gb, gbt, act_s, gh_s, live, weight,
    dm_acc, dm_land, late_acc, late_stage, late_land, late_split, late_parts, late_sum, late_rows, late_near, late_far, dvec, sums, hid_s, pul_s, n1_send, n1_recv, n1_rows,
    sem_x, sem_cot, sem_w, sem_out, sem_ig, sem_dm, send_sems, recv_sems,
    dm_send, dm_recv, late_send, late_recv, n1_ssem, n1_rsem,
):
    grid, feats = sz.grid, sz.feats
    chunks, subs = sz.chunks, sz.subs
    me = lax.axis_index("grid")
    index = {"batch": lax.axis_index("batch"), "grid": me}
    hi_v, lo_v = n2, gb
    modes = sz.modes
    groups = feats // 128
    mix_rows = 4 * groups * BSIZE
    blocks = sz.hidden // FT
    order = [("batch", b) for b in range(batch_bits)] + [("grid", b) for b in range(grid_bits)]
    swapped = list(order)
    if grid_bits > 1:
        swapped[batch_bits], swapped[batch_bits + 1] = swapped[batch_bits + 1], swapped[batch_bits]

    for c in range(chunks):
        pltpu.make_async_copy(x_hbm.at[c], x_v.at[c], sem_x.at[c]).start()
    for c in range(chunks):
        pltpu.make_async_copy(cot_hbm.at[c], cot_v.at[c], sem_cot.at[c]).start()
    load_win = pltpu.make_async_copy(win_hbm, w_in, sem_w.at[0])
    load_wout = pltpu.make_async_copy(wout_hbm, w_out, sem_w.at[1])
    load_win.start()
    load_wout.start()

    barrier = pltpu.get_barrier_semaphore()

    def other(k):
        batch = 2**batch_bits
        b = lax.rem(index["batch"] + k // grid, batch)
        g = lax.rem(me + lax.rem(k, grid), grid)
        return {"batch": b, "grid": g}

    everyone = 2**batch_bits * grid

    @pl.loop(1, everyone)
    def _(k):
        pl.semaphore_signal(barrier, inc=1, device_id=other(k), device_id_type=MESH)

    def exchange(stage, c, send, recv):
        @pl.loop(0, grid - 1)
        def _(j):
            k = grid // 2 + ((j + 1) // 2) * (2 * lax.rem(j + 1, 2) - 1)
            peer = lax.rem(me + k, grid)
            pltpu.make_async_remote_copy(
                src_ref=send.at[c, peer],
                dst_ref=recv.at[c, me],
                send_sem=send_sems.at[stage, c],
                recv_sem=recv_sems.at[stage, c],
                device_id={"grid": peer},
                device_id_type=MESH,
            ).start()

        recv[c, me] = send[c, me]

    def arrived(stage, c, recv):
        part = recv.at[c, pl.ds(0, grid - 1)]
        pltpu.make_async_copy(part, part, recv_sems.at[stage, c]).wait()

    def sent(stage, c, send):
        part = send.at[c, pl.ds(0, grid - 1)]
        pltpu.make_async_copy(part, part, send_sems.at[stage, c]).wait()

    def doubled(rows, inner):
        mode = lax.rem(lax.broadcasted_iota(jnp.int32, (rows, 1), 0) // inner, sz.own)
        return jnp.where(mode + me * sz.own == 0, 1.0, 2.0).astype(F32)

    def row_tile(t):
        return pl.ds(pl.multiple_of(t * TILE, TILE), TILE)

    def mix_tile(j, t):
        return pl.ds(pl.multiple_of(j * sz.modes + t * TILE, TILE), TILE)

    def lanes(j):
        return pl.ds(128 * j, 128)

    def wide(j):
        return pl.ds(256 * j, 256)

    def send_columns(c, table, send):
        for s in range(subs):
            cells = pl.ds(s * sz.sub_cells, sz.sub_cells)
            high = hi_v[cells, :]
            out = dot(table[0], high) + dot(table[0], lo_v[cells, :]) + dot(table[1], high)
            send[c, :, s] = out.astype(BF16).reshape(grid, 16, feats)

    def both_parts(ref, j):
        return jnp.concatenate([ref[0, :, lanes(j)], ref[1, :, lanes(j)]], axis=1)

    def bias_parts(ref, j):
        return jnp.concatenate([ref[0:1, lanes(j)], ref[1:2, lanes(j)]], axis=1)

    @pl.loop(0, chunks)
    def _(c):
        pltpu.make_async_copy(x_hbm.at[c], x_v.at[c], sem_x.at[c]).wait()

        @each_tile(CELLS)
        def _(t):
            xhat, scale = moments(x_v[c, row_tile(t), :].astype(F32))
            hi_v[row_tile(t), :], lo_v[row_tile(t), :] = split(xhat * gain1[...] + bias1[...])

        send_columns(c, t_f, send_a)

        @pl.when(c == 0)
        def _():
            pl.semaphore_wait(barrier, everyone - 1)

        exchange(0, c, send_a, recv_a)


    pick_row = lax.broadcasted_iota(jnp.int32, (BSIZE, 128), 0)
    pick_lane = lax.broadcasted_iota(jnp.int32, (BSIZE, 128), 1)
    picks = [(pick_lane == pick_row + BSIZE * side).astype(F32).astype(BF16) for side in range(2)]
    for raw, big in ((sw1, w1), (sw2, w2)):
        for j in range(groups):
            real, imag = [
                jnp.concatenate([dot(raw[r, 2 * j + side], picks[side]) for side in range(2)], axis=0) for r in range(2)
            ]
            big[j, :128, :128] = real.astype(BF16)
            big[j, :128, 128:] = imag.astype(BF16)
            big[j, 128:, :128] = (-imag).astype(BF16)
            big[j, 128:, 128:] = real.astype(BF16)

    width = feats // masks.shape[0]

    @pl.loop(0, sz.items)
    def _(i):
        kind = ids[i]
        for g in range(masks.shape[0]):
            live[i, :, pl.ds(g * width, width)] = jnp.full((1, width), masks[g, kind].astype(F32))
        weight[i] = jnp.full((1, feats), counts[kind].astype(F32) * 0.125)

    for s in range(dm_acc.shape[0]):

        def clear(o, n):
            dm_acc[s, pl.ds(o, n), :] = jnp.zeros((n, feats), F32)

        tiled(dm_acc.shape[1], clear)
    dw1[...] = jnp.zeros_like(dw1)
    dw2[...] = jnp.zeros_like(dw2)
    dvec[...] = jnp.zeros_like(dvec)
    sums[...] = jnp.zeros_like(sums)

    @pl.loop(0, chunks)
    def _(c):
        arrived(0, c, recv_a)
        for s in range(subs):
            got = recv_a[c, :, s].reshape(grid * 16, feats)
            out = (dot(t_rf[0], got) + dot(t_rf[1], got)).astype(BF16)
            at = pl.ds(s * sz.sub_modes, sz.sub_modes)
            spec[c, 0, at, :] = out[: sz.sub_modes]
            spec[c, 1, at, :] = out[sz.sub_modes :]
        for j in range(groups):
            pul_s[pl.ds(j * sz.modes, sz.modes), :256] = dot(both_parts(spec.at[c], j), w1[j])
        for j in range(groups):

            @each_tile(sz.modes)
            def _(t):
                at = row_tile(t)
                act, slope = gelu_parts(pul_s[mix_tile(j, t), :256] + bias_parts(sb1, j))
                act1[c, at, wide(j)] = act.astype(BF16)
                slope1[c, at, wide(j)] = slope

        for j in range(groups):
            pul_s[pl.ds(j * sz.modes, sz.modes), :256] = dot(act1[c, :, wide(j)], w2[j])
        for j in range(groups):

            @each_tile(sz.modes)
            def _(t):
                at = row_tile(t)
                mixed = pul_s[mix_tile(j, t), :256] + bias_parts(sb2, j)
                bend = jnp.tanh(mixed * (1.0 / SHRINK))
                slope2[c, at, wide(j)] = bend * bend
                shrunk = (mixed - SHRINK * bend).astype(BF16)
                gbt[mix_tile(0, t), lanes(j)] = shrunk[:, :128]
                gbt[mix_tile(1, t), lanes(j)] = shrunk[:, 128:]

        for s in range(subs):
            at = pl.ds(s * sz.sub_modes, sz.sub_modes)
            second, third, fourth = [pl.ds(k * modes + s * sz.sub_modes, sz.sub_modes) for k in (1, 2, 3)]
            high = jnp.concatenate([gbt[at, :], gbt[second, :]], axis=0)
            out = (dot(t_rb[0], high) + dot(t_rb[1], high)) * doubled(grid * 16, 2)
            send_b[c, :, s] = out.astype(BF16).reshape(grid, 16, feats)
        exchange(1, c, send_b, recv_b)

    load_win.wait()
    load_wout.wait()

    def feed_forward(c):
        pltpu.make_async_copy(cot_hbm.at[c], cot_v.at[c], sem_cot.at[c]).wait()
        arrived(1, c, recv_b)
        for s in range(subs):
            cells = pl.ds(s * sz.sub_cells, sz.sub_cells)
            got = recv_b[c, :, s].reshape(grid * 16, feats)
            gres[c, cells, :] = dot(t_b[0], got) + dot(t_b[1], got)

        @each_tile(CELLS)
        def _(t):
            at = row_tile(t)
            item = c * sz.chunk_items + (t * TILE) // sz.item_cells
            total = x_v[c, at, :].astype(F32) + live[item] * gres[c, at, :]
            gres[c, at, :] = total
            xhat, scale = moments(total)
            n2[at, :] = (xhat * gain2[...] + bias2[...]).astype(BF16)
            grad = (cot_v[c, at, :].astype(F32) * weight[item]).astype(BF16)
            gb[at, :] = grad
            sums[BOUT] += eight_rows(grad.astype(F32))

        n2t[...] = n2[...].T
        gbt[...] = gb[...].T

        def products(f):
            at = pl.ds(f * FT, FT)
            hid_s[...] = dot(n2[...], w_in[:, at])
            pul_s[...] = dot_nt(gb[...], w_out[at, :])

        for f in range(blocks):
            products(f)
            at = pl.ds(f * FT, FT)

            @each_tile(CELLS)
            def _(t):
                rows = row_tile(t)
                act, slope = gelu_parts(hid_s[rows, :] + b_in[:, at])
                act_s[rows, at] = act.astype(BF16)
                grad = (slope * pul_s[rows, :]).astype(BF16)
                gh_s[rows, at] = grad
                sums[BIN + f] += eight_rows(grad.astype(F32))

        hid_s[...] = dot_nt(gh_s[...], w_in[...])
        pul_s[...] = dot(act_s[...], w_out[...])

        @each_tile(CELLS)
        def _(t):
            at = row_tile(t)
            item = c * sz.chunk_items + (t * TILE) // sz.item_cells
            total = gres[c, at, :]
            xhat, scale = moments(total)
            grad = hid_s[at, :]
            sums[GAIN2] += eight_rows(grad * xhat)
            sums[BIAS2] += eight_rows(grad)
            grad_out = cot_v[c, at, :].astype(F32) * weight[item]
            cot_v[c, at, :] = (total + pul_s[at, :] + b_out[...]).astype(BF16)
            out = grad_out + pull_norm(grad, xhat, scale, gain2[...])
            gres[c, at, :] = out
            hi_v[at, :], lo_v[at, :] = split(out * live[item])

        sent(0, c, send_a)
        send_columns(c, t_f, send_a)
        exchange(2, c, send_a, recv_a)
        pltpu.make_async_copy(cot_v.at[c], act_hbm.at[c], sem_out.at[c]).start()
        for f in range(blocks):
            at, into = pl.ds(f * FT, FT), pl.ds((f % 2) * feats, feats)
            dm_acc[f // 2, into, :] += dot(n2t[...], gh_s[:, at])
            dm_acc[blocks // 2 + f // 2, into, :] += dot(gbt[...], act_s[:, at])

    def dz_of(j):
        return n2t[pl.ds((j // 2) * modes, modes), wide(j % 2)]

    def dm_of(j):
        return n2t[pl.ds((2 + j // 2) * modes, modes), wide(j % 2)]

    def mix_backward(c):
        arrived(2, c, recv_a)
        for s in range(subs):
            got = recv_a[c, :, s].reshape(grid * 16, feats)
            out = (dot(t_rf[0], got) + dot(t_rf[1], got)) * doubled(2 * sz.sub_modes, MODES)
            at = pl.ds(s * sz.sub_modes, sz.sub_modes)
            hid_s[at, :] = out[: sz.sub_modes]
            hid_s[pl.ds(sz.modes + s * sz.sub_modes, sz.sub_modes), :] = out[sz.sub_modes :]
        for j in range(groups):

            @each_tile(sz.modes)
            def _(t):
                at = row_tile(t)
                low_at = pl.ds(pl.multiple_of(sz.modes + t * TILE, TILE), TILE)
                both = jnp.concatenate([hid_s[at, lanes(j)], hid_s[low_at, lanes(j)]], axis=1)
                dz = (both * slope2[c, at, wide(j)]).astype(BF16)
                n2t[mix_tile(j // 2, t), wide(j % 2)] = dz
                dz = eight_rows(dz.astype(F32))
                for r in range(2):
                    sums[SB2 + r, :, lanes(j)] += dz[:, 128 * r : 128 * r + 128]

        for j in range(groups):
            pul_s[pl.ds(j * sz.modes, sz.modes), :256] = dot_nt(dz_of(j), w2[j])
        for j in range(groups):

            @each_tile(sz.modes)
            def _(t):
                at = row_tile(t)
                dm = (pul_s[mix_tile(j, t), :256] * slope1[c, at, wide(j)]).astype(BF16)
                n2t[mix_tile(2 + j // 2, t), wide(j % 2)] = dm
                dm = eight_rows(dm.astype(F32))
                for r in range(2):
                    sums[SB1 + r, :, lanes(j)] += dm[:, 128 * r : 128 * r + 128]

        for j in range(groups):
            pul_s[pl.ds(j * sz.modes, sz.modes), :256] = dot_nt(dm_of(j), w1[j])
        for j in range(groups):

            @each_tile(sz.modes)
            def _(t):
                at = row_tile(t)
                high, low = split(pul_s[mix_tile(j, t), :256])
                for r in range(2):
                    gbt[mix_tile(r, t), lanes(j)] = high[:, 128 * r : 128 * r + 128]
                    gbt[mix_tile(2 + r, t), lanes(j)] = low[:, 128 * r : 128 * r + 128]

        sent(1, c, send_b)
        for s in range(subs):
            at = pl.ds(s * sz.sub_modes, sz.sub_modes)
            second, third, fourth = [pl.ds(k * modes + s * sz.sub_modes, sz.sub_modes) for k in (1, 2, 3)]
            high = jnp.concatenate([gbt[at, :], gbt[second, :]], axis=0)
            low = jnp.concatenate([gbt[third, :], gbt[fourth, :]], axis=0)
            out = dot(t_rb[0], high) + dot(t_rb[0], low) + dot(t_rb[1], high)
            send_b[c, :, s] = out.astype(BF16).reshape(grid, 16, feats)
        exchange(3, c, send_b, recv_b)
        for j in range(groups):
            dz, dm = dz_of(j), dm_of(j)
            dw2[j] += dot_tn(act1[c, :, wide(j)], dz)
            dw1[j] += dot_tn(both_parts(spec.at[c], j), dm)

    def near_of(s, off, size):
        return w_in.at[pl.ds(pl.multiple_of(off, 16), size), pl.ds(s * FT, FT)]

    def near_mixing(off, size):
        return ds_near.at[pl.ds(pl.multiple_of(off, 16), size)]

    segments = [
        Reducer(
            dm_acc.at[s], (act_s.at[:, pl.ds(s * FT, FT)], gh_s.at[:, pl.ds(s * FT, FT)]), dm_land.at[s], functools.partial(near_of, s),
            dm_send.at[s], dm_recv.at[s], order if s < blocks // 2 else swapped, index,
        )
        for s in range(blocks)
    ]

    def all_of(group, k):
        for one in group:
            one.ticks()[k]()

    mix_piece, vec_piece = mix_rows // (2 * grid), 16 * groups // (2 * grid)
    half_side = lax.rem(index["batch"], 2)
    plane, planes = sz.plane, sz.planes
    my_z, my_p = me // plane, lax.rem(me, plane)

    def partner(bit):
        side = lax.rem(index["batch"] // 2**bit, 2)
        return {"batch": index["batch"] + (1 - 2 * side) * 2**bit}

    def late_copy(step, source, target, device):
        return pltpu.make_async_remote_copy(
            src_ref=source, dst_ref=target, send_sem=late_send.at[step], recv_sem=late_recv.at[step],
            device_id=device, device_id_type=MESH,
        )

    def late_halves(bit):
        return late_copy(bit, late_stage.at[bit], late_land.at[bit], partner(bit))

    def late_plane(step, k):
        p = lax.rem(my_p + k, plane)
        device = {"grid": my_z * plane + p}
        if step == batch_bits:
            return late_copy(step, late_split.at[:, p], late_parts.at[my_p], device)
        return late_copy(step, late_near.at[:, my_p], late_near.at[:, my_p], device)

    def late_z(step, k):
        z = lax.rem(my_z + k, planes)
        device = {"grid": z * plane + my_p}
        if step == batch_bits + 1:
            return late_copy(step, late_sum.at[z], late_rows.at[my_z], device)
        return late_copy(step, late_near.at[my_z, my_p], late_near.at[my_z, my_p], device)

    def late_home():
        return late_copy(batch_bits + 4, late_near, late_far, partner(0))

    def late_first():
        late_acc[...] = jnp.zeros_like(late_acc)
        for layer, big in enumerate((dw1, dw2)):
            for j in range(groups):
                real = big[j, :128, :128] + big[j, 128:, 128:]
                imag = big[j, :128, 128:] - big[j, 128:, :128]
                for r, part in enumerate((real, imag)):
                    part = jnp.where(pick_lane < BSIZE, part[:BSIZE], part[BSIZE:])
                    for o in range(0, BSIZE, mix_piece):
                        row = ((layer * 2 + r) * groups + j) * BSIZE + o
                        n = min(mix_piece, BSIZE)
                        piece, into = row // mix_piece, row % mix_piece
                        late_acc[piece // grid, piece % grid, into : into + n, :] = part[o : o + n]
        for row in range(SB1, 16):
            dvec[row : row + 1, :] = jnp.sum(sums[row], axis=0, keepdims=True)
        vectors = jnp.concatenate([dvec[:, lanes(j)] for j in range(groups)], axis=0)
        for piece in range(2 * grid):
            late_acc[piece // grid, piece % grid, mix_piece : mix_piece + vec_piece, :] = vectors[
                piece * vec_piece : (piece + 1) * vec_piece
            ]
        late_stage[0] = late_acc[1 - half_side].astype(BF16)
        late_halves(0).start()

    def late_second():
        late_halves(0).wait_recv()
        total = late_acc[half_side] + late_land[0].astype(F32)
        for bit in range(1, batch_bits):
            late_stage[bit] = total.astype(BF16)
            late_halves(bit).start()
            late_halves(bit).wait_recv()
            total = late_stage[bit].astype(F32) + late_land[bit].astype(F32)
        late_split[...] = total.astype(BF16).reshape(late_split.shape)

        @pl.loop(1, plane)
        def _(k):
            late_plane(batch_bits, k).start()

    def late_wait(part, step):
        pltpu.make_async_copy(part, part, late_recv.at[step]).wait()

    def late_third():
        late_wait(late_parts.at[pl.ds(0, plane - 1)], batch_bits)
        late_parts[my_p] = late_split[:, my_p]
        total = late_parts[0].astype(F32)
        for k in range(1, plane):
            total = total + late_parts[k].astype(F32)
        late_sum[...] = total.astype(BF16)

        @pl.loop(1, planes)
        def _(k):
            late_z(batch_bits + 1, k).start()

    def late_fourth():
        late_wait(late_rows.at[pl.ds(0, planes - 1)], batch_bits + 1)
        late_rows[my_z] = late_sum[my_z]
        total = late_rows[0].astype(F32)
        for k in range(1, planes):
            total = total + late_rows[k].astype(F32)
        late_near[my_z, my_p] = total.astype(BF16)

        @pl.loop(1, planes)
        def _(k):
            late_z(batch_bits + 2, k).start()

    def late_fifth():
        late_wait(late_near.at[pl.ds(0, planes - 1), my_p], batch_bits + 2)

        @pl.loop(1, plane)
        def _(k):
            late_plane(batch_bits + 3, k).start()

    def late_sixth():
        late_wait(late_near.at[:, pl.ds(0, plane - 1)], batch_bits + 3)
        late_home().start()

    def late_seventh():
        late_home().wait_recv()

    def late_sent():
        for bit in range(batch_bits):
            late_halves(bit).wait_send()

        @pl.loop(1, plane)
        def _(k):
            late_plane(batch_bits, k).wait_send()
            late_plane(batch_bits + 3, k).wait_send()

        @pl.loop(1, planes)
        def _(k):
            late_z(batch_bits + 1, k).wait_send()
            late_z(batch_bits + 2, k).wait_send()

        late_home().wait_send()

    queues = {
        "e": [functools.partial(all_of, segments[0::2], k) for k in range(len(segments[0].ticks()))],
        "f": [functools.partial(all_of, segments[1::2], k) for k in range(len(segments[0].ticks()))],
        "l": [late_first, late_second, late_third, late_fourth, late_fifth, late_sixth, late_seventh],
    }

    def run(names):
        for name in names:
            if queues[name]:
                queues[name].pop(0)()

    def finish_inputs(c):
        arrived(3, c, recv_b)
        for s in range(subs):
            cells = pl.ds(s * sz.sub_cells, sz.sub_cells)
            got = recv_b[c, :, s].reshape(grid * 16, feats)
            hid_s[cells, :] = dot(t_b[0], got) + dot(t_b[1], got)

        @each_tile(CELLS)
        def _(t):
            at = row_tile(t)
            xhat, scale = moments(x_v[c, at, :].astype(F32))
            grad = hid_s[at, :]
            sums[GAIN1] += eight_rows(grad * xhat)
            sums[BIAS1] += eight_rows(grad)
            gres[c, at, :] += pull_norm(grad, xhat, scale, gain1[...])

        pltpu.make_async_copy(gres.at[c], ig_hbm.at[c], sem_ig.at[c]).start()

    @pl.loop(0, 2 * chunks)
    def _(c):
        @pl.when(c < chunks)
        def _():
            feed_forward(c)

        @pl.when(c == chunks - 1)
        def _():
            run("ef")

        @pl.when(jnp.logical_and(c >= 2, c < chunks + 2))
        def _():
            mix_backward(c - 2)

        @pl.when(c == chunks - 1)
        def _():
            run("e")

        @pl.when(c == chunks)
        def _():
            run("fe")

        @pl.when(c == chunks + 1)
        def _():
            run("l")

        @pl.when(c >= chunks)
        def _():
            finish_inputs(c - chunks)

        for k, names in enumerate(("fe", "felfe", "felfelfel")[: chunks - 1]):

            @pl.when(c == chunks + k)
            def _():
                run(names)

    last = [jnp.sum(sums[row], axis=0, keepdims=True) for row in (GAIN1, BIAS1)]
    own = jnp.concatenate([last[k % 2][:, 128 * (k // 2) : 128 * (k // 2) + 128] for k in range(2 * groups)], axis=0)
    near_count = 2**batch_bits * plane
    n1_send[0] = own
    n1_recv[index["batch"] * plane + my_p] = own

    def n1_near(k):
        device = {
            "batch": lax.rem(index["batch"] + k // plane, 2**batch_bits),
            "grid": my_z * plane + lax.rem(my_p + lax.rem(k, plane), plane),
        }
        return pltpu.make_async_remote_copy(
            src_ref=n1_send.at[0], dst_ref=n1_recv.at[index["batch"] * plane + my_p], send_sem=n1_ssem.at[0],
            recv_sem=n1_rsem.at[0], device_id=device, device_id_type=MESH,
        )

    def n1_far(k):
        return pltpu.make_async_remote_copy(
            src_ref=n1_send.at[1], dst_ref=n1_rows.at[my_z], send_sem=n1_ssem.at[1], recv_sem=n1_rsem.at[1],
            device_id={"grid": lax.rem(my_z + k, planes) * plane + my_p}, device_id_type=MESH,
        )

    def n1_wait(part, step):
        pltpu.make_async_copy(part, part, n1_rsem.at[step]).wait()

    @pl.loop(1, near_count)
    def _(k):
        n1_near(k).start()

    run("le")
    n1_wait(n1_recv.at[pl.ds(0, near_count - 1)], 0)
    total = n1_recv[0]
    for k in range(1, near_count):
        total = total + n1_recv[k]
    n1_send[1] = total
    n1_rows[my_z] = total

    @pl.loop(1, planes)
    def _(k):
        n1_far(k).start()

    while any(queues.values()):
        run("lef")
    for side, held in enumerate((late_near, late_far)):
        place = half_side if side == 0 else 1 - half_side
        dspec_out[place] = held[:, :, :mix_piece, :].reshape(mix_rows // 2, 128)
        for g in range(grid):
            late_acc[place, g, mix_piece : mix_piece + vec_piece, :] = held[
                g // plane, g % plane, mix_piece : mix_piece + vec_piece, :
            ].astype(F32)
    for piece in range(2 * grid):
        for k in range(vec_piece):
            row = piece * vec_piece + k
            dvec_out[row % 16, lanes(row // 16)] = late_acc[piece // grid, piece % grid, mix_piece + k, :]
    n1_wait(n1_rows.at[pl.ds(0, planes - 1)], 1)
    total = n1_rows[0]
    for k in range(1, planes):
        total = total + n1_rows[k]
    for j in range(groups):
        dvec_out[0:2, lanes(j)] = total[2 * j : 2 * j + 2, :]

    outs = []
    halves_of = blocks // 2
    for half, turned in zip(range(halves_of), (n2, n2t)):
        near_in, near_out = [pl.ds((half + m * halves_of) * FT, FT) for m in range(2)]
        outs.append(pltpu.make_async_copy(w_in.at[:, near_in], near_hbm.at[half], sem_dm.at[half]))
        outs[-1].start()
        turned[...] = w_in[:, near_out].T
        outs.append(pltpu.make_async_copy(turned, near_hbm.at[halves_of + half], sem_dm.at[halves_of + half]))
        outs[-1].start()

    for one in segments:
        one.wait_sent()
    late_sent()

    @pl.loop(1, near_count)
    def _(k):
        n1_near(k).wait_send()

    @pl.loop(1, planes)
    def _(k):
        n1_far(k).wait_send()

    @pl.loop(0, chunks)
    def _(c):
        sent(2, c, send_a)
        sent(3, c, send_b)
        pltpu.make_async_copy(cot_v.at[c], act_hbm.at[c], sem_out.at[c]).wait()
        pltpu.make_async_copy(gres.at[c], ig_hbm.at[c], sem_ig.at[c]).wait()

    for copy in outs:
        copy.wait()


def finish(
    sz,
    act_in, ig_in, near_in, dspec, dvec,
    act_hbm, ig_hbm, gain1, bias1, sw1, sb1, sw2, sb2, gain2, bias2, dmi_hbm, b_in, dmo_hbm, b_out,
    act_v, ig_v, near_v, near_f, sem_in, sem_out,
):
    chunks, feats, hidden = sz.chunks, sz.feats, sz.hidden
    widened = widen(near_in, near_v, near_f, dmi_hbm, dmo_hbm, lax.rem(lax.axis_index("batch"), 2), sem_in, sem_out)
    moves = []
    for c in range(chunks):
        for m, (source, held, target) in enumerate(((ig_in, ig_v, ig_hbm), (act_in, act_v, act_hbm))):
            k = 2 * near_v.shape[0] + 2 * c + m
            moves.append(
                (
                    pltpu.make_async_copy(source.at[c], held.at[c], sem_in.at[k]),
                    pltpu.make_async_copy(held.at[c], target.at[c], sem_out.at[k]),
                )
            )
    next(widened)
    for fetch, store in moves:
        fetch.start()
    for layer, out in enumerate((sw1, sw2)):
        for side in range(2):
            row = lax.broadcasted_iota(jnp.int32, (128, BSIZE), 0)
            lane = lax.broadcasted_iota(jnp.int32, (128, BSIZE), 1)
            pick = (row == lane + BSIZE * side).astype(F32).astype(BF16)
            picked = dot(dspec[layer], pick)
            for r in range(2):
                for j in range(BLOCKS // 2):
                    at = (r * (BLOCKS // 2) + j) * BSIZE
                    out[r, 2 * j + side] = picked[at : at + BSIZE]
    for row, out in ((GAIN1, gain1), (BIAS1, bias1), (GAIN2, gain2), (BIAS2, bias2), (BOUT, b_out)):
        out[...] = dvec[row : row + 1, :]
    sb1[...] = dvec[SB1 : SB1 + 2, :]
    sb2[...] = dvec[SB2 : SB2 + 2, :]
    for f in range(hidden // feats):
        b_in[:, f * feats : (f + 1) * feats] = dvec[BIN + f : BIN + f + 1, :]
    next(widened)
    for fetch, store in moves:
        fetch.wait()
        store.start()
    for fetch, store in moves:
        store.wait()
    for _ in widened:
        pass


def widen(source, held, wide, dmi_hbm, dmo_hbm, side, sem_in, sem_out):
    halves_of, feats = source.shape[0] // 2, source.shape[1]
    rows = feats // 2
    moves = []
    for block in range(2 * halves_of):
        at = pl.ds(pl.multiple_of((2 * (block % halves_of) + side) * FT, FT), FT)
        for part in range(2):
            here = pl.ds(part * rows, rows)
            if block < halves_of:
                target = dmi_hbm.at[here, at]
            else:
                target = dmo_hbm.at[pl.ds(pl.multiple_of((2 * (block % halves_of) + side) * FT + part * rows, rows), rows)]
            k = 2 * block + part
            moves.append(
                (
                    pltpu.make_async_copy(source.at[block, here], held.at[block, here], sem_in.at[k]),
                    pltpu.make_async_copy(wide.at[block, here], target, sem_out.at[k]), block, here,
                )
            )
    for fetch, store, block, here in moves:
        fetch.start()
    yield
    for fetch, store, block, here in moves:
        fetch.wait()
        for o in range(0, rows, COPY):
            at = pl.ds(here.start + o, COPY)
            wide[block, at, :] = held[block, at, :].astype(F32)
        store.start()
    yield
    for fetch, store, block, here in moves:
        store.wait()


def finish_far(far_in, dmi_in, dmo_in, dmi_hbm, dmo_hbm, far_v, far_f, sem_in, sem_out):
    side = 1 - lax.rem(lax.axis_index("batch"), 2)
    for _ in widen(far_in, far_v, far_f, dmi_hbm, dmo_hbm, side, sem_in, sem_out):
        pass


def local(
    batch, grid,
    inputs, cotangent, dataset_ids, channel_masks, sample_counts, norm1_gain, norm1_bias,
    spec_w1, spec_b1, spec_w2, spec_b2, norm2_gain, norm2_bias, mlp_in, mlp_in_bias, mlp_out, mlp_out_bias,
):
    items, rows, cols, feats = inputs.shape
    hidden = mlp_in.shape[1]
    sz = sizes_of(items, rows, cols, feats, hidden, grid)
    batch_bits, grid_bits = batch.bit_length() - 1, grid.bit_length() - 1
    bits = batch_bits + grid_bits

    vmem = pl.BlockSpec(memory_space=pltpu.VMEM)
    smem = pl.BlockSpec(memory_space=pltpu.SMEM)
    hbm = pl.BlockSpec(memory_space=pl.ANY)
    chunks, groups, blocks = sz.chunks, feats // 128, hidden // FT
    shape = (chunks, CELLS, feats)
    pieces = (chunks, grid, sz.subs, 16, feats)
    seg_rows = 2 * feats
    mix_rows = 4 * groups * BSIZE
    late = (grid, mix_rows // (2 * grid) + 16, 128)
    plane, planes = sz.plane, sz.planes
    out_shape = (
        jax.ShapeDtypeStruct(shape, BF16),
        jax.ShapeDtypeStruct(shape, F32),
        jax.ShapeDtypeStruct((blocks, feats, FT), BF16),
        jax.ShapeDtypeStruct((2, mix_rows // 2, 128), BF16),
        jax.ShapeDtypeStruct((16, feats), F32),
    )
    dma = pltpu.SemaphoreType.DMA
    scratch = [
        pltpu.VMEM(shape, BF16),
        pltpu.VMEM(shape, BF16),
        pltpu.VMEM(mlp_in.shape, BF16),
        pltpu.VMEM(mlp_out.shape, BF16),
        *[pltpu.VMEM(pieces, BF16)] * 4,
        pltpu.VMEM(shape, F32),
        pltpu.VMEM((chunks, 2, sz.modes, feats), BF16),
        pltpu.VMEM((chunks, sz.modes, 2 * feats), BF16),
        pltpu.VMEM((chunks, sz.modes, 2 * feats), F32),
        pltpu.VMEM((chunks, sz.modes, 2 * feats), F32),
        pltpu.VMEM((groups, 256, 256), BF16),
        pltpu.VMEM((groups, 256, 256), BF16),
        pltpu.VMEM((groups, 256, 256), F32),
        pltpu.VMEM((groups, 256, 256), F32),
        pltpu.VMEM((CELLS, feats), BF16),
        pltpu.VMEM((feats, CELLS), BF16),
        pltpu.VMEM((CELLS, feats), BF16),
        pltpu.VMEM((feats, CELLS), BF16),
        pltpu.VMEM((CELLS, hidden), BF16),
        pltpu.VMEM((CELLS, hidden), BF16),
        pltpu.VMEM((items, 1, feats), F32),
        pltpu.VMEM((items, 1, feats), F32),
        pltpu.VMEM((blocks, seg_rows, FT), F32),
        pltpu.VMEM((blocks, landing_rows(seg_rows, bits), FT), BF16),
        pltpu.VMEM((2, *late), F32),
        pltpu.VMEM((batch_bits, *late), BF16),
        pltpu.VMEM((batch_bits, *late), BF16),
        pltpu.VMEM((planes, plane, *late[1:]), BF16),
        pltpu.VMEM((plane, planes, *late[1:]), BF16),
        pltpu.VMEM((planes, *late[1:]), BF16),
        pltpu.VMEM((planes, *late[1:]), BF16),
        *[pltpu.VMEM((planes, plane, *late[1:]), BF16)] * 2,
        pltpu.VMEM((16, feats), F32),
        pltpu.VMEM((16, 8, feats), F32),
        pltpu.VMEM((CELLS, FT), F32),
        pltpu.VMEM((CELLS, FT), F32),
        pltpu.VMEM((2, 2 * groups, 128), F32),
        pltpu.VMEM((batch * plane, 2 * groups, 128), F32),
        pltpu.VMEM((planes, 2 * groups, 128), F32),
        dma((chunks,)),
        dma((chunks,)),
        dma((2,)),
        dma((chunks,)),
        dma((chunks,)),
        dma((blocks,)),
        *[dma((4, chunks))] * 2,
        dma((blocks, 2 * bits)),
        dma((blocks, 2 * bits)),
        dma((batch_bits + 5,)),
        dma((batch_bits + 5,)),
        dma((2,)),
        dma((2,)),
    ]
    cells = items * rows * cols
    row = lambda v: v.reshape(1, -1)
    parts = pl.pallas_call(
        functools.partial(kernel, sz, batch_bits, grid_bits),
        out_shape=out_shape,
        in_specs=[smem] * 3 + [hbm, hbm] + [vmem] * 14 + [hbm, hbm],
        out_specs=(hbm, hbm, hbm, vmem, vmem),
        scratch_shapes=scratch,
        cost_estimate=pl.CostEstimate(
            flops=14 * cells * feats * hidden, bytes_accessed=24 << 20, transcendentals=3 * cells * hidden
        ),
        compiler_params=pltpu.CompilerParams(
            collective_id=0, has_side_effects=True, vmem_limit_bytes=67_000_000
        ),
    )(
        dataset_ids, channel_masks.T, sample_counts,
        inputs.reshape(shape), cotangent.reshape(shape),
        row(norm1_gain), row(norm1_bias), row(norm2_gain), row(norm2_bias),
        spec_w1, spec_b1, spec_w2, spec_b2, row(mlp_in_bias), row(mlp_out_bias),
        *[jnp.asarray(t) for t in tables(sz)], mlp_in, mlp_out,
    )
    vector = jax.ShapeDtypeStruct((1, feats), F32)
    pair = jax.ShapeDtypeStruct((2, feats), F32)
    mixers = jax.ShapeDtypeStruct(spec_w1.shape, F32)
    moves = 2 * blocks + 2 * chunks
    half_shape = (blocks, feats, FT)
    outs = pl.pallas_call(
        functools.partial(finish, sz),
        out_shape=(
            out_shape[0], out_shape[1], vector, vector, mixers, pair, mixers, pair, vector, vector,
            jax.ShapeDtypeStruct(mlp_in.shape, F32), jax.ShapeDtypeStruct((1, hidden), F32),
            jax.ShapeDtypeStruct(mlp_out.shape, F32), vector,
        ),
        in_specs=[hbm] * 3 + [vmem] * 2,
        out_specs=(hbm, hbm) + (vmem,) * 8 + (hbm, vmem, hbm, vmem),
        scratch_shapes=[
            pltpu.VMEM(shape, BF16), pltpu.VMEM(shape, F32), pltpu.VMEM(half_shape, BF16), pltpu.VMEM(half_shape, F32),
            dma((moves,)), dma((moves,)),
        ],
        cost_estimate=pl.CostEstimate(flops=0, bytes_accessed=24 << 20, transcendentals=0),
        compiler_params=pltpu.CompilerParams(vmem_limit_bytes=67_000_000),
    )(*parts)
    far = lax.ppermute(parts[2], "batch", [(b, b ^ 1) for b in range(batch)])
    wide = (jax.ShapeDtypeStruct(mlp_in.shape, F32), jax.ShapeDtypeStruct(mlp_out.shape, F32))
    dmi, dmo = pl.pallas_call(
        finish_far,
        out_shape=wide,
        in_specs=[hbm] * 3,
        out_specs=(hbm, hbm),
        input_output_aliases={1: 0, 2: 1},
        scratch_shapes=[
            pltpu.VMEM(half_shape, BF16), pltpu.VMEM(half_shape, F32), dma((2 * blocks,)), dma((2 * blocks,)),
        ],
        cost_estimate=pl.CostEstimate(flops=0, bytes_accessed=6 << 20, transcendentals=0),
        compiler_params=pltpu.CompilerParams(vmem_limit_bytes=67_000_000),
    )(far, outs[10], outs[12])
    flat = lambda v: v.reshape(-1)
    return (
        outs[0].reshape(inputs.shape), outs[1].reshape(inputs.shape), flat(outs[2]), flat(outs[3]), *outs[4:8],
        flat(outs[8]), flat(outs[9]), dmi, flat(outs[11]), dmo, flat(outs[13]),
    )


def solution(mesh):
    spread = P("batch", "grid", None, None)
    return jax.shard_map(
        functools.partial(local, mesh.shape["batch"], mesh.shape["grid"]),
        mesh=mesh,
        in_specs=(spread, spread, P("batch")) + (P(),) * 14,
        out_specs=(spread, spread) + (P(),) * 12,
        check_vma=False,
    )
```

```python
import functools
import math

import jax
import jax.numpy as jnp
import numpy as np
from jax import lax
from jax.experimental import pallas as pl
from jax.experimental.pallas import tpu as pltpu
from jax.sharding import PartitionSpec as P

BLOCKS = 8
MODES = 32
BSIZE = 64
EPSILON = 1e-06
SHRINK = 0.1
MESH = pl.DeviceIdType.MESH
F32 = jnp.float32
BF16 = jnp.bfloat16
CELLS = 512
TILE = 16
COPY = 32
FT = 512


def sizes_of(items, rows, cols, feats, hidden, grid):
    sz = type("Sizes", (), {})()
    sz.items, sz.rows, sz.cols, sz.feats, sz.hidden, sz.grid = items, rows, cols, feats, hidden, grid
    sz.own = MODES // grid
    sz.plane = math.gcd(grid, 4)
    sz.planes = grid // sz.plane
    sz.height = rows * grid
    sz.item_cells = rows * cols
    sz.sub_items = 16 // (rows * sz.own * 2)
    sz.sub_cells = sz.sub_items * sz.item_cells
    sz.subs = CELLS // sz.sub_cells
    sz.chunk_items = sz.subs * sz.sub_items
    sz.chunks = items // sz.chunk_items
    sz.sub_modes = sz.sub_items * sz.own * MODES
    sz.modes = sz.subs * sz.sub_modes
    return sz


def halves(table):
    high = table.astype(BF16)
    low = (table - high.astype(np.float64)).astype(BF16)
    return np.stack([high, low])


def tables(sz):
    its, rows, own, cols, grid = sz.sub_items, sz.rows, sz.own, sz.cols, sz.grid
    w = np.arange(cols)
    q = np.arange(MODES)
    angle = 2 * np.pi * (np.outer(q, w) % cols) / cols
    col = np.stack([np.cos(angle), -np.sin(angle)], axis=1) / math.sqrt(cols)
    lines = its * rows
    eye = np.eye(lines)

    def placed(tab):
        tab = tab.reshape(grid, own, 2, cols)
        big = np.einsum("gqrw,lm->glqrmw", tab, eye)
        return big.reshape(grid * 16, lines * cols)

    first = placed(col)
    p = np.where(q < MODES // 2, q, sz.height - MODES + q)
    h = np.arange(sz.height)
    angle = 2 * np.pi * (np.outer(p, h) % sz.height) / sz.height
    cosine, sine = np.cos(angle), np.sin(angle)
    row = np.stack([np.stack([cosine, sine], -1), np.stack([-sine, cosine], -1)], 1) / math.sqrt(sz.height)
    row = row.reshape(MODES, 2, grid, rows, 2)
    big = np.einsum("psghr,ij,qk->siqpgjhkr", row, np.eye(its), np.eye(own))
    big = big.reshape(2 * sz.sub_modes, grid * 16)
    return [halves(t) for t in (first, first.T, big, big.T)]


def dot(a, b):
    return jnp.dot(a, b, preferred_element_type=F32)


def dot_nt(a, b):
    return lax.dot_general(a, b, (((1,), (1,)), ((), ())), preferred_element_type=F32)


def dot_tn(a, b):
    return lax.dot_general(a, b, (((0,), (0,)), ((), ())), preferred_element_type=F32)


def split(v):
    high = v.astype(BF16)
    return high, (v - high.astype(F32)).astype(BF16)


CDF = (
    0.797884941492634, 0.03633308439449127, -3.259472654998994e-05, -5.530632529808752e-05, 3.964774886835927e-06,
    -1.3226642974616402e-07, 1.756281964154736e-09,
)


def gelu_parts(v):
    square = v * v
    inner = jnp.minimum(square, 30.0)
    q = CDF[6] * inner + CDF[5]
    for coef in CDF[4::-1]:
        q = q * inner + coef
    cdf = 0.5 + 0.5 * jnp.tanh(v * q)
    pdf = jnp.exp2(square * (-0.5 * math.log2(math.e))) * (1.0 / math.sqrt(2.0 * math.pi))
    return v * cdf, cdf + v * pdf


def moments(v):
    centred = v - jnp.mean(v, axis=-1, keepdims=True)
    scale = lax.rsqrt(jnp.mean(centred * centred, axis=-1, keepdims=True) + EPSILON)
    return centred * scale, scale


def pull_norm(grad, xhat, scale, gain):
    gy = grad * gain
    return (gy - jnp.mean(gy, -1, keepdims=True) - xhat * jnp.mean(gy * xhat, -1, keepdims=True)) * scale


def eight_rows(v):
    return jnp.sum(v.reshape(v.shape[0] // 8, 8, v.shape[1]), axis=0)


GAIN1, BIAS1, SB1, SB2, GAIN2, BIAS2, BOUT, BIN = 0, 1, 2, 4, 6, 7, 8, 9


def tiled(count, body):
    size = min(count, COPY)

    @pl.loop(0, count // size, unroll=min(4, count // size))
    def _(t):
        body(t * size, size)


def each_tile(rows):
    return pl.loop(0, rows // TILE, unroll=rows // TILE)


def landing_rows(rows, bits):
    total = 0
    for _ in range(bits):
        rows = rows // 2 if rows % 32 == 0 else rows
        total += rows
    return total


class Pieces:
    def __init__(self, source, target, rows, send_sem, recv_sem, device):
        self.source, self.target, self.rows, self.device = source, target, rows, device
        self.send_sem, self.recv_sem = send_sem, recv_sem

    def part(self, at):
        return pltpu.make_async_remote_copy(
            src_ref=self.source.at[at], dst_ref=self.target.at[at], send_sem=self.send_sem, recv_sem=self.recv_sem,
            device_id=self.device, device_id_type=MESH,
        )

    def start(self):
        size = max(16, self.rows // 8)

        @pl.loop(0, self.rows // size)
        def _(k):
            self.part(pl.ds(pl.multiple_of(k * size, 16), size)).start()

    def wait_send(self):
        self.part(pl.ds(0, self.rows)).wait_send()

    def wait_recv(self):
        self.part(pl.ds(0, self.rows)).wait_recv()


class Reducer:
    def __init__(self, acc, stages, landing, near, send_sems, recv_sems, order, index):
        self.acc, self.stages, self.landing, self.near = acc, stages, landing, near
        self.send_sems, self.recv_sems = send_sems, recv_sems
        self.steps = []
        size, off, land = acc.shape[0], 0, 0
        for axis, bit in order:
            side = lax.rem(index[axis] // 2**bit, 2)
            partner = {axis: index[axis] + (1 - 2 * side) * 2**bit}
            halving = size % 32 == 0
            if halving:
                size = size // 2
                away, off = off + (1 - side) * size, off + side * size
            else:
                away = off
            self.steps.append((halving, size, away, off, land, partner))
            land += size
        self.off, self.size = off, size
        self.back = [k for k in reversed(range(1, len(order))) if self.steps[k][0]]

    def at(self, off, size):
        return pl.ds(pl.multiple_of(off, 16), size)

    def stage(self, k):
        halving, size, away, off, land, partner = self.steps[k]
        if not halving:
            return self.near(off - self.steps[0][3], size)
        return self.stages[0] if k == 0 else self.stages[1].at[pl.ds(land - self.steps[0][1], size)]

    def copy(self, k):
        halving, size, away, off, land, partner = self.steps[k]
        return Pieces(
            self.stage(k), self.landing.at[pl.ds(land, size)], size, self.send_sems.at[k], self.recv_sems.at[k], partner
        )

    def start(self, k):
        halving, size, away, off, land, partner = self.steps[k]

        stage = self.stage(k)

        def body(o, n):
            stage[pl.ds(o, n), :] = self.acc[self.at(away + o, n), :].astype(BF16)

        tiled(size, body)
        self.copy(k).start()

    def finish(self, k):
        halving, size, away, off, land, partner = self.steps[k]
        self.copy(k).wait_recv()
        if not halving:
            self.copy(k).wait_send()
        stage = self.stage(k)

        def body(o, n):
            at = self.at(off + o, n)
            mine = self.acc[at, :] if halving else stage[pl.ds(o, n), :].astype(F32)
            self.acc[at, :] = mine + self.landing[pl.ds(land + o, n), :].astype(F32)

        tiled(size, body)

    def begin_back(self):
        first = self.steps[0][3]

        def body(o, n):
            at = self.at(self.off + o, n)
            self.near(self.off - first + o, n)[...] = self.acc[at, :].astype(BF16)

        tiled(self.size, body)

    def back_copy(self, i):
        halving, size, away, off, land, partner = self.steps[self.back[i]]
        part = self.near(off - self.steps[0][3], size)
        sem = len(self.steps) + i
        return Pieces(part, part, size, self.send_sems.at[sem], self.recv_sems.at[sem], partner)

    def ticks(self):
        count, back = len(self.steps), len(self.back)

        def first():
            self.start(0)

        def forth(k):
            self.finish(k)
            if k + 1 < count:
                self.start(k + 1)
            else:
                self.begin_back()
                self.back_copy(0).start()

        def home(i):
            self.back_copy(i).wait_recv()
            if i + 1 < back:
                self.back_copy(i + 1).start()

        return (
            [first]
            + [functools.partial(forth, k) for k in range(count)]
            + [functools.partial(home, i) for i in range(back)]
        )

    def wait_sent(self):
        for k, step in enumerate(self.steps):
            if step[0]:
                self.copy(k).wait_send()
        for i in range(len(self.back)):
            self.back_copy(i).wait_send()


def kernel(
    sz, batch_bits, grid_bits,
    ids, masks, counts,
    x_hbm, cot_hbm, gain1, bias1, gain2, bias2, sw1, sb1, sw2, sb2, b_in, b_out,
    t_f, t_b, t_rf, t_rb, win_hbm, wout_hbm,
    act_hbm, ig_hbm, near_hbm, dspec_out, dvec_out,
    x_v, cot_v, w_in, w_out, send_a, recv_a, send_b, recv_b, gres,
    spec, act1, slope1, slope2, w1, w2, dw1, dw2,
    n2, n2t, gb, gbt, act_s, gh_s, live, weight,
    dm_acc, dm_land, late_acc, late_stage, late_land, late_split, late_parts, late_sum, late_rows, late_near, late_far, dvec, sums, hid_s, pul_s, n1_send, n1_recv, n1_rows,
    sem_x, sem_cot, sem_w, sem_out, sem_ig, sem_dm, send_sems, recv_sems,
    dm_send, dm_recv, late_send, late_recv, n1_ssem, n1_rsem,
):
    grid, feats = sz.grid, sz.feats
    chunks, subs = sz.chunks, sz.subs
    me = lax.axis_index("grid")
    index = {"batch": lax.axis_index("batch"), "grid": me}
    hi_v, lo_v = n2, gb
    modes = sz.modes
    groups = feats // 128
    mix_rows = 4 * groups * BSIZE
    blocks = sz.hidden // FT
    order = [("batch", b) for b in range(batch_bits)] + [("grid", b) for b in range(grid_bits)]
    swapped = list(order)
    if grid_bits > 1:
        swapped[batch_bits], swapped[batch_bits + 1] = swapped[batch_bits + 1], swapped[batch_bits]

    for c in range(chunks):
        pltpu.make_async_copy(x_hbm.at[c], x_v.at[c], sem_x.at[c]).start()
    for c in range(chunks):
        pltpu.make_async_copy(cot_hbm.at[c], cot_v.at[c], sem_cot.at[c]).start()
    load_win = pltpu.make_async_copy(win_hbm, w_in, sem_w.at[0])
    load_wout = pltpu.make_async_copy(wout_hbm, w_out, sem_w.at[1])
    load_win.start()
    load_wout.start()

    barrier = pltpu.get_barrier_semaphore()

    def other(k):
        batch = 2**batch_bits
        b = lax.rem(index["batch"] + k // grid, batch)
        g = lax.rem(me + lax.rem(k, grid), grid)
        return {"batch": b, "grid": g}

    everyone = 2**batch_bits * grid

    @pl.loop(1, everyone)
    def _(k):
        pl.semaphore_signal(barrier, inc=1, device_id=other(k), device_id_type=MESH)

    ranked = sorted(range(1, grid), key=lambda k: abs(k - grid // 2))
    turns = [ranked[j // 2] if j % 2 == 0 else ranked[-1 - j // 2] for j in range(grid - 1)]

    def exchange(stage, c, send, recv):
        for k in turns:
            peer = lax.rem(me + k, grid)
            pltpu.make_async_remote_copy(
                src_ref=send.at[c, peer],
                dst_ref=recv.at[c, me],
                send_sem=send_sems.at[stage, c],
                recv_sem=recv_sems.at[stage, c],
                device_id={"grid": peer},
                device_id_type=MESH,
            ).start()

        recv[c, me] = send[c, me]

    def arrived(stage, c, recv):
        part = recv.at[c, pl.ds(0, grid - 1)]
        pltpu.make_async_copy(part, part, recv_sems.at[stage, c]).wait()

    def sent(stage, c, send):
        part = send.at[c, pl.ds(0, grid - 1)]
        pltpu.make_async_copy(part, part, send_sems.at[stage, c]).wait()

    def doubled(rows, inner):
        mode = lax.rem(lax.broadcasted_iota(jnp.int32, (rows, 1), 0) // inner, sz.own)
        return jnp.where(mode + me * sz.own == 0, 1.0, 2.0).astype(F32)

    def row_tile(t):
        return pl.ds(pl.multiple_of(t * TILE, TILE), TILE)

    def mix_tile(j, t):
        return pl.ds(pl.multiple_of(j * sz.modes + t * TILE, TILE), TILE)

    def lanes(j):
        return pl.ds(128 * j, 128)

    def wide(j):
        return pl.ds(256 * j, 256)

    def send_columns(c, table, send):
        for s in range(subs):
            cells = pl.ds(s * sz.sub_cells, sz.sub_cells)
            high = hi_v[cells, :]
            out = dot(table[0], high) + dot(table[0], lo_v[cells, :]) + dot(table[1], high)
            send[c, :, s] = out.astype(BF16).reshape(grid, 16, feats)

    def both_parts(ref, j):
        return jnp.concatenate([ref[0, :, lanes(j)], ref[1, :, lanes(j)]], axis=1)

    def bias_parts(ref, j):
        return jnp.concatenate([ref[0:1, lanes(j)], ref[1:2, lanes(j)]], axis=1)

    @pl.loop(0, chunks)
    def _(c):
        pltpu.make_async_copy(x_hbm.at[c], x_v.at[c], sem_x.at[c]).wait()

        @each_tile(CELLS)
        def _(t):
            xhat, scale = moments(x_v[c, row_tile(t), :].astype(F32))
            hi_v[row_tile(t), :], lo_v[row_tile(t), :] = split(xhat * gain1[...] + bias1[...])

        send_columns(c, t_f, send_a)

        @pl.when(c == 0)
        def _():
            pl.semaphore_wait(barrier, everyone - 1)

        exchange(0, c, send_a, recv_a)


    pick_row = lax.broadcasted_iota(jnp.int32, (BSIZE, 128), 0)
    pick_lane = lax.broadcasted_iota(jnp.int32, (BSIZE, 128), 1)
    picks = [(pick_lane == pick_row + BSIZE * side).astype(F32).astype(BF16) for side in range(2)]
    for raw, big in ((sw1, w1), (sw2, w2)):
        for j in range(groups):
            real, imag = [
                jnp.concatenate([dot(raw[r, 2 * j + side], picks[side]) for side in range(2)], axis=0) for r in range(2)
            ]
            big[j, :128, :128] = real.astype(BF16)
            big[j, :128, 128:] = imag.astype(BF16)
            big[j, 128:, :128] = (-imag).astype(BF16)
            big[j, 128:, 128:] = real.astype(BF16)

    width = feats // masks.shape[0]

    @pl.loop(0, sz.items)
    def _(i):
        kind = ids[i]
        for g in range(masks.shape[0]):
            live[i, :, pl.ds(g * width, width)] = jnp.full((1, width), masks[g, kind].astype(F32))
        weight[i] = jnp.full((1, feats), counts[kind].astype(F32) * 0.125)

    for s in range(dm_acc.shape[0]):

        def clear(o, n):
            dm_acc[s, pl.ds(o, n), :] = jnp.zeros((n, feats), F32)

        tiled(dm_acc.shape[1], clear)
    dw1[...] = jnp.zeros_like(dw1)
    dw2[...] = jnp.zeros_like(dw2)
    dvec[...] = jnp.zeros_like(dvec)
    sums[...] = jnp.zeros_like(sums)

    @pl.loop(0, chunks)
    def _(c):
        arrived(0, c, recv_a)
        for s in range(subs):
            got = recv_a[c, :, s].reshape(grid * 16, feats)
            out = (dot(t_rf[0], got) + dot(t_rf[1], got)).astype(BF16)
            at = pl.ds(s * sz.sub_modes, sz.sub_modes)
            spec[c, 0, at, :] = out[: sz.sub_modes]
            spec[c, 1, at, :] = out[sz.sub_modes :]
        for j in range(groups):
            pul_s[pl.ds(j * sz.modes, sz.modes), :256] = dot(both_parts(spec.at[c], j), w1[j])
        for j in range(groups):

            @each_tile(sz.modes)
            def _(t):
                at = row_tile(t)
                act, slope = gelu_parts(pul_s[mix_tile(j, t), :256] + bias_parts(sb1, j))
                act1[c, at, wide(j)] = act.astype(BF16)
                slope1[c, at, wide(j)] = slope

        for j in range(groups):
            pul_s[pl.ds(j * sz.modes, sz.modes), :256] = dot(act1[c, :, wide(j)], w2[j])
        for j in range(groups):

            @each_tile(sz.modes)
            def _(t):
                at = row_tile(t)
                mixed = pul_s[mix_tile(j, t), :256] + bias_parts(sb2, j)
                bend = jnp.tanh(mixed * (1.0 / SHRINK))
                slope2[c, at, wide(j)] = bend * bend
                shrunk = (mixed - SHRINK * bend).astype(BF16)
                gbt[mix_tile(0, t), lanes(j)] = shrunk[:, :128]
                gbt[mix_tile(1, t), lanes(j)] = shrunk[:, 128:]

        for s in range(subs):
            at = pl.ds(s * sz.sub_modes, sz.sub_modes)
            second, third, fourth = [pl.ds(k * modes + s * sz.sub_modes, sz.sub_modes) for k in (1, 2, 3)]
            high = jnp.concatenate([gbt[at, :], gbt[second, :]], axis=0)
            out = (dot(t_rb[0], high) + dot(t_rb[1], high)) * doubled(grid * 16, 2)
            send_b[c, :, s] = out.astype(BF16).reshape(grid, 16, feats)
        exchange(1, c, send_b, recv_b)

    load_win.wait()
    load_wout.wait()

    def feed_forward(c):
        pltpu.make_async_copy(cot_hbm.at[c], cot_v.at[c], sem_cot.at[c]).wait()
        arrived(1, c, recv_b)
        for s in range(subs):
            cells = pl.ds(s * sz.sub_cells, sz.sub_cells)
            got = recv_b[c, :, s].reshape(grid * 16, feats)
            gres[c, cells, :] = dot(t_b[0], got) + dot(t_b[1], got)

        @each_tile(CELLS)
        def _(t):
            at = row_tile(t)
            item = c * sz.chunk_items + (t * TILE) // sz.item_cells
            total = x_v[c, at, :].astype(F32) + live[item] * gres[c, at, :]
            gres[c, at, :] = total
            xhat, scale = moments(total)
            n2[at, :] = (xhat * gain2[...] + bias2[...]).astype(BF16)
            grad = (cot_v[c, at, :].astype(F32) * weight[item]).astype(BF16)
            gb[at, :] = grad
            sums[BOUT] += eight_rows(grad.astype(F32))

        n2t[...] = n2[...].T
        gbt[...] = gb[...].T

        def products(f):
            at = pl.ds(f * FT, FT)
            hid_s[...] = dot(n2[...], w_in[:, at])
            pul_s[...] = dot_nt(gb[...], w_out[at, :])

        for f in range(blocks):
            products(f)
            at = pl.ds(f * FT, FT)

            @each_tile(CELLS)
            def _(t):
                rows = row_tile(t)
                act, slope = gelu_parts(hid_s[rows, :] + b_in[:, at])
                act_s[rows, at] = act.astype(BF16)
                grad = (slope * pul_s[rows, :]).astype(BF16)
                gh_s[rows, at] = grad
                sums[BIN + f] += eight_rows(grad.astype(F32))

        hid_s[...] = dot_nt(gh_s[...], w_in[...])
        pul_s[...] = dot(act_s[...], w_out[...])

        @each_tile(CELLS)
        def _(t):
            at = row_tile(t)
            item = c * sz.chunk_items + (t * TILE) // sz.item_cells
            total = gres[c, at, :]
            xhat, scale = moments(total)
            grad = hid_s[at, :]
            sums[GAIN2] += eight_rows(grad * xhat)
            sums[BIAS2] += eight_rows(grad)
            grad_out = cot_v[c, at, :].astype(F32) * weight[item]
            cot_v[c, at, :] = (total + pul_s[at, :] + b_out[...]).astype(BF16)
            out = grad_out + pull_norm(grad, xhat, scale, gain2[...])
            gres[c, at, :] = out
            hi_v[at, :], lo_v[at, :] = split(out * live[item])

        sent(0, c, send_a)
        send_columns(c, t_f, send_a)
        exchange(2, c, send_a, recv_a)
        pltpu.make_async_copy(cot_v.at[c], act_hbm.at[c], sem_out.at[c]).start()
        for f in range(blocks):
            at, into = pl.ds(f * FT, FT), pl.ds((f % 2) * feats, feats)
            dm_acc[f // 2, into, :] += dot(n2t[...], gh_s[:, at])
            dm_acc[blocks // 2 + f // 2, into, :] += dot(gbt[...], act_s[:, at])

    def dz_of(j):
        return n2t[pl.ds((j // 2) * modes, modes), wide(j % 2)]

    def dm_of(j):
        return n2t[pl.ds((2 + j // 2) * modes, modes), wide(j % 2)]

    def mix_backward(c):
        arrived(2, c, recv_a)
        for s in range(subs):
            got = recv_a[c, :, s].reshape(grid * 16, feats)
            out = (dot(t_rf[0], got) + dot(t_rf[1], got)) * doubled(2 * sz.sub_modes, MODES)
            at = pl.ds(s * sz.sub_modes, sz.sub_modes)
            hid_s[at, :] = out[: sz.sub_modes]
            hid_s[pl.ds(sz.modes + s * sz.sub_modes, sz.sub_modes), :] = out[sz.sub_modes :]
        for j in range(groups):

            @each_tile(sz.modes)
            def _(t):
                at = row_tile(t)
                low_at = pl.ds(pl.multiple_of(sz.modes + t * TILE, TILE), TILE)
                both = jnp.concatenate([hid_s[at, lanes(j)], hid_s[low_at, lanes(j)]], axis=1)
                dz = (both * slope2[c, at, wide(j)]).astype(BF16)
                n2t[mix_tile(j // 2, t), wide(j % 2)] = dz
                dz = eight_rows(dz.astype(F32))
                for r in range(2):
                    sums[SB2 + r, :, lanes(j)] += dz[:, 128 * r : 128 * r + 128]

        for j in range(groups):
            pul_s[pl.ds(j * sz.modes, sz.modes), :256] = dot_nt(dz_of(j), w2[j])
        for j in range(groups):

            @each_tile(sz.modes)
            def _(t):
                at = row_tile(t)
                dm = (pul_s[mix_tile(j, t), :256] * slope1[c, at, wide(j)]).astype(BF16)
                n2t[mix_tile(2 + j // 2, t), wide(j % 2)] = dm
                dm = eight_rows(dm.astype(F32))
                for r in range(2):
                    sums[SB1 + r, :, lanes(j)] += dm[:, 128 * r : 128 * r + 128]

        for j in range(groups):
            pul_s[pl.ds(j * sz.modes, sz.modes), :256] = dot_nt(dm_of(j), w1[j])
        for j in range(groups):

            @each_tile(sz.modes)
            def _(t):
                at = row_tile(t)
                high, low = split(pul_s[mix_tile(j, t), :256])
                for r in range(2):
                    gbt[mix_tile(r, t), lanes(j)] = high[:, 128 * r : 128 * r + 128]
                    gbt[mix_tile(2 + r, t), lanes(j)] = low[:, 128 * r : 128 * r + 128]

        sent(1, c, send_b)
        for s in range(subs):
            at = pl.ds(s * sz.sub_modes, sz.sub_modes)
            second, third, fourth = [pl.ds(k * modes + s * sz.sub_modes, sz.sub_modes) for k in (1, 2, 3)]
            high = jnp.concatenate([gbt[at, :], gbt[second, :]], axis=0)
            low = jnp.concatenate([gbt[third, :], gbt[fourth, :]], axis=0)
            out = dot(t_rb[0], high) + dot(t_rb[0], low) + dot(t_rb[1], high)
            send_b[c, :, s] = out.astype(BF16).reshape(grid, 16, feats)
        exchange(3, c, send_b, recv_b)
        for j in range(groups):
            dz, dm = dz_of(j), dm_of(j)
            dw2[j] += dot_tn(act1[c, :, wide(j)], dz)
            dw1[j] += dot_tn(both_parts(spec.at[c], j), dm)

    def near_of(s, off, size):
        return w_in.at[pl.ds(pl.multiple_of(off, 16), size), pl.ds(s * FT, FT)]

    def near_mixing(off, size):
        return ds_near.at[pl.ds(pl.multiple_of(off, 16), size)]

    segments = [
        Reducer(
            dm_acc.at[s], (act_s.at[:, pl.ds(s * FT, FT)], gh_s.at[:, pl.ds(s * FT, FT)]), dm_land.at[s], functools.partial(near_of, s),
            dm_send.at[s], dm_recv.at[s], order if s < blocks // 2 else swapped, index,
        )
        for s in range(blocks)
    ]

    def all_of(group, k):
        for one in group:
            one.ticks()[k]()

    mix_piece, vec_piece = mix_rows // (2 * grid), 16 * groups // (2 * grid)
    half_side = lax.rem(index["batch"], 2)
    plane, planes = sz.plane, sz.planes
    my_z, my_p = me // plane, lax.rem(me, plane)

    def partner(bit):
        side = lax.rem(index["batch"] // 2**bit, 2)
        return {"batch": index["batch"] + (1 - 2 * side) * 2**bit}

    def late_copy(step, source, target, device):
        return pltpu.make_async_remote_copy(
            src_ref=source, dst_ref=target, send_sem=late_send.at[step], recv_sem=late_recv.at[step],
            device_id=device, device_id_type=MESH,
        )

    def late_halves(bit):
        return late_copy(bit, late_stage.at[bit], late_land.at[bit], partner(bit))

    def late_plane(step, k):
        p = lax.rem(my_p + k, plane)
        device = {"grid": my_z * plane + p}
        if step == batch_bits:
            return late_copy(step, late_split.at[:, p], late_parts.at[my_p], device)
        return late_copy(step, late_near.at[:, my_p], late_near.at[:, my_p], device)

    def late_z(step, k):
        z = lax.rem(my_z + k, planes)
        device = {"grid": z * plane + my_p}
        if step == batch_bits + 1:
            return late_copy(step, late_sum.at[z], late_rows.at[my_z], device)
        return late_copy(step, late_near.at[my_z, my_p], late_near.at[my_z, my_p], device)

    def late_home():
        return late_copy(batch_bits + 4, late_near, late_far, partner(0))

    def late_first():
        late_acc[...] = jnp.zeros_like(late_acc)
        for layer, big in enumerate((dw1, dw2)):
            for j in range(groups):
                real = big[j, :128, :128] + big[j, 128:, 128:]
                imag = big[j, :128, 128:] - big[j, 128:, :128]
                for r, part in enumerate((real, imag)):
                    part = jnp.where(pick_lane < BSIZE, part[:BSIZE], part[BSIZE:])
                    for o in range(0, BSIZE, mix_piece):
                        row = ((layer * 2 + r) * groups + j) * BSIZE + o
                        n = min(mix_piece, BSIZE)
                        piece, into = row // mix_piece, row % mix_piece
                        late_acc[piece // grid, piece % grid, into : into + n, :] = part[o : o + n]
        for row in range(SB1, 16):
            dvec[row : row + 1, :] = jnp.sum(sums[row], axis=0, keepdims=True)
        vectors = jnp.concatenate([dvec[:, lanes(j)] for j in range(groups)], axis=0)
        for piece in range(2 * grid):
            late_acc[piece // grid, piece % grid, mix_piece : mix_piece + vec_piece, :] = vectors[
                piece * vec_piece : (piece + 1) * vec_piece
            ]
        late_stage[0] = late_acc[1 - half_side].astype(BF16)
        late_halves(0).start()

    def late_second():
        late_halves(0).wait_recv()
        total = late_acc[half_side] + late_land[0].astype(F32)
        for bit in range(1, batch_bits):
            late_stage[bit] = total.astype(BF16)
            late_halves(bit).start()
            late_halves(bit).wait_recv()
            total = late_stage[bit].astype(F32) + late_land[bit].astype(F32)
        late_split[...] = total.astype(BF16).reshape(late_split.shape)

        @pl.loop(1, plane)
        def _(k):
            late_plane(batch_bits, k).start()

    def late_wait(part, step):
        pltpu.make_async_copy(part, part, late_recv.at[step]).wait()

    def late_third():
        late_wait(late_parts.at[pl.ds(0, plane - 1)], batch_bits)
        late_parts[my_p] = late_split[:, my_p]
        total = late_parts[0].astype(F32)
        for k in range(1, plane):
            total = total + late_parts[k].astype(F32)
        late_sum[...] = total.astype(BF16)

        @pl.loop(1, planes)
        def _(k):
            late_z(batch_bits + 1, k).start()

    def late_fourth():
        late_wait(late_rows.at[pl.ds(0, planes - 1)], batch_bits + 1)
        late_rows[my_z] = late_sum[my_z]
        total = late_rows[0].astype(F32)
        for k in range(1, planes):
            total = total + late_rows[k].astype(F32)
        late_near[my_z, my_p] = total.astype(BF16)

        @pl.loop(1, planes)
        def _(k):
            late_z(batch_bits + 2, k).start()

    def late_fifth():
        late_wait(late_near.at[pl.ds(0, planes - 1), my_p], batch_bits + 2)

        @pl.loop(1, plane)
        def _(k):
            late_plane(batch_bits + 3, k).start()

    def late_sixth():
        late_wait(late_near.at[:, pl.ds(0, plane - 1)], batch_bits + 3)
        late_home().start()

    def late_seventh():
        late_home().wait_recv()

    def late_sent():
        for bit in range(batch_bits):
            late_halves(bit).wait_send()

        @pl.loop(1, plane)
        def _(k):
            late_plane(batch_bits, k).wait_send()
            late_plane(batch_bits + 3, k).wait_send()

        @pl.loop(1, planes)
        def _(k):
            late_z(batch_bits + 1, k).wait_send()
            late_z(batch_bits + 2, k).wait_send()

        late_home().wait_send()

    queues = {
        "e": [functools.partial(all_of, segments[0::2], k) for k in range(len(segments[0].ticks()))],
        "f": [functools.partial(all_of, segments[1::2], k) for k in range(len(segments[0].ticks()))],
        "l": [late_first, late_second, late_third, late_fourth, late_fifth, late_sixth, late_seventh],
    }

    def run(names):
        for name in names:
            if queues[name]:
                queues[name].pop(0)()

    def finish_inputs(c):
        arrived(3, c, recv_b)
        for s in range(subs):
            cells = pl.ds(s * sz.sub_cells, sz.sub_cells)
            got = recv_b[c, :, s].reshape(grid * 16, feats)
            hid_s[cells, :] = dot(t_b[0], got) + dot(t_b[1], got)

        @each_tile(CELLS)
        def _(t):
            at = row_tile(t)
            xhat, scale = moments(x_v[c, at, :].astype(F32))
            grad = hid_s[at, :]
            sums[GAIN1] += eight_rows(grad * xhat)
            sums[BIAS1] += eight_rows(grad)
            gres[c, at, :] += pull_norm(grad, xhat, scale, gain1[...])

        pltpu.make_async_copy(gres.at[c], ig_hbm.at[c], sem_ig.at[c]).start()

    @pl.loop(0, 2 * chunks)
    def _(c):
        @pl.when(c < chunks)
        def _():
            feed_forward(c)

        @pl.when(c == chunks - 1)
        def _():
            run("ef")

        @pl.when(jnp.logical_and(c >= 2, c < chunks + 2))
        def _():
            mix_backward(c - 2)

        @pl.when(c == chunks - 1)
        def _():
            run("e")

        @pl.when(c == chunks)
        def _():
            run("fe")

        @pl.when(c == chunks + 1)
        def _():
            run("l")

        @pl.when(c >= chunks)
        def _():
            finish_inputs(c - chunks)

        for k, names in enumerate(("fe", "felfe", "felfelfel")[: chunks - 1]):

            @pl.when(c == chunks + k)
            def _():
                run(names)

    last = [jnp.sum(sums[row], axis=0, keepdims=True) for row in (GAIN1, BIAS1)]
    own = jnp.concatenate([last[k % 2][:, 128 * (k // 2) : 128 * (k // 2) + 128] for k in range(2 * groups)], axis=0)
    near_count = 2**batch_bits * plane
    n1_send[0] = own
    n1_recv[index["batch"] * plane + my_p] = own

    def n1_near(k):
        device = {
            "batch": lax.rem(index["batch"] + k // plane, 2**batch_bits),
            "grid": my_z * plane + lax.rem(my_p + lax.rem(k, plane), plane),
        }
        return pltpu.make_async_remote_copy(
            src_ref=n1_send.at[0], dst_ref=n1_recv.at[index["batch"] * plane + my_p], send_sem=n1_ssem.at[0],
            recv_sem=n1_rsem.at[0], device_id=device, device_id_type=MESH,
        )

    def n1_far(k):
        return pltpu.make_async_remote_copy(
            src_ref=n1_send.at[1], dst_ref=n1_rows.at[my_z], send_sem=n1_ssem.at[1], recv_sem=n1_rsem.at[1],
            device_id={"grid": lax.rem(my_z + k, planes) * plane + my_p}, device_id_type=MESH,
        )

    def n1_wait(part, step):
        pltpu.make_async_copy(part, part, n1_rsem.at[step]).wait()

    @pl.loop(1, near_count)
    def _(k):
        n1_near(k).start()

    run("le")
    n1_wait(n1_recv.at[pl.ds(0, near_count - 1)], 0)
    total = n1_recv[0]
    for k in range(1, near_count):
        total = total + n1_recv[k]
    n1_send[1] = total
    n1_rows[my_z] = total

    @pl.loop(1, planes)
    def _(k):
        n1_far(k).start()

    while any(queues.values()):
        run("lef")
    for side, held in enumerate((late_near, late_far)):
        place = half_side if side == 0 else 1 - half_side
        dspec_out[place] = held[:, :, :mix_piece, :].reshape(mix_rows // 2, 128)
        for g in range(grid):
            late_acc[place, g, mix_piece : mix_piece + vec_piece, :] = held[
                g // plane, g % plane, mix_piece : mix_piece + vec_piece, :
            ].astype(F32)
    for piece in range(2 * grid):
        for k in range(vec_piece):
            row = piece * vec_piece + k
            dvec_out[row % 16, lanes(row // 16)] = late_acc[piece // grid, piece % grid, mix_piece + k, :]
    n1_wait(n1_rows.at[pl.ds(0, planes - 1)], 1)
    total = n1_rows[0]
    for k in range(1, planes):
        total = total + n1_rows[k]
    for j in range(groups):
        dvec_out[0:2, lanes(j)] = total[2 * j : 2 * j + 2, :]

    outs = []
    halves_of = blocks // 2
    for half, turned in zip(range(halves_of), (n2, n2t)):
        near_in, near_out = [pl.ds((half + m * halves_of) * FT, FT) for m in range(2)]
        outs.append(pltpu.make_async_copy(w_in.at[:, near_in], near_hbm.at[half], sem_dm.at[half]))
        outs[-1].start()
        turned[...] = w_in[:, near_out].T
        outs.append(pltpu.make_async_copy(turned, near_hbm.at[halves_of + half], sem_dm.at[halves_of + half]))
        outs[-1].start()

    for one in segments:
        one.wait_sent()
    late_sent()

    @pl.loop(1, near_count)
    def _(k):
        n1_near(k).wait_send()

    @pl.loop(1, planes)
    def _(k):
        n1_far(k).wait_send()

    @pl.loop(0, chunks)
    def _(c):
        sent(2, c, send_a)
        sent(3, c, send_b)
        pltpu.make_async_copy(cot_v.at[c], act_hbm.at[c], sem_out.at[c]).wait()
        pltpu.make_async_copy(gres.at[c], ig_hbm.at[c], sem_ig.at[c]).wait()

    for copy in outs:
        copy.wait()


def finish(
    sz,
    act_in, ig_in, near_in, dspec_in, dvec_in,
    act_hbm, ig_hbm, gain1, bias1, sw1, sb1, sw2, sb2, gain2, bias2, dmi_hbm, b_in, dmo_hbm, b_out,
    act_v, ig_v, near_v, near_f, dspec, dvec, sem_in, sem_out, sem_small,
):
    chunks, feats, hidden = sz.chunks, sz.feats, sz.hidden
    small = [
        pltpu.make_async_copy(source, held, sem_small.at[k])
        for k, (source, held) in enumerate(((dspec_in, dspec), (dvec_in, dvec)))
    ]
    for copy in small:
        copy.start()
    widened = widen(near_in, near_v, near_f, dmi_hbm, dmo_hbm, lax.rem(lax.axis_index("batch"), 2), sem_in, sem_out)
    moves = []
    for c in range(chunks):
        for m, (source, held, target) in enumerate(((ig_in, ig_v, ig_hbm), (act_in, act_v, act_hbm))):
            k = 2 * near_v.shape[0] + 2 * c + m
            moves.append(
                (
                    pltpu.make_async_copy(source.at[c], held.at[c], sem_in.at[k]),
                    pltpu.make_async_copy(held.at[c], target.at[c], sem_out.at[k]),
                )
            )
    next(widened)
    for fetch, store in moves:
        fetch.start()
    for copy in small:
        copy.wait()
    for layer, out in enumerate((sw1, sw2)):
        for side in range(2):
            row = lax.broadcasted_iota(jnp.int32, (128, BSIZE), 0)
            lane = lax.broadcasted_iota(jnp.int32, (128, BSIZE), 1)
            pick = (row == lane + BSIZE * side).astype(F32).astype(BF16)
            picked = dot(dspec[layer], pick)
            for r in range(2):
                for j in range(BLOCKS // 2):
                    at = (r * (BLOCKS // 2) + j) * BSIZE
                    out[r, 2 * j + side] = picked[at : at + BSIZE]
    for row, out in ((GAIN1, gain1), (BIAS1, bias1), (GAIN2, gain2), (BIAS2, bias2), (BOUT, b_out)):
        out[...] = dvec[row : row + 1, :]
    sb1[...] = dvec[SB1 : SB1 + 2, :]
    sb2[...] = dvec[SB2 : SB2 + 2, :]
    for f in range(hidden // feats):
        b_in[:, f * feats : (f + 1) * feats] = dvec[BIN + f : BIN + f + 1, :]
    next(widened)
    for fetch, store in moves:
        fetch.wait()
        store.start()
    for fetch, store in moves:
        store.wait()
    for _ in widened:
        pass


def widen(source, held, wide, dmi_hbm, dmo_hbm, side, sem_in, sem_out):
    halves_of, feats = source.shape[0] // 2, source.shape[1]
    rows = feats // 2
    moves = []
    for block in range(2 * halves_of):
        at = pl.ds(pl.multiple_of((2 * (block % halves_of) + side) * FT, FT), FT)
        for part in range(2):
            here = pl.ds(part * rows, rows)
            if block < halves_of:
                target = dmi_hbm.at[here, at]
            else:
                target = dmo_hbm.at[pl.ds(pl.multiple_of((2 * (block % halves_of) + side) * FT + part * rows, rows), rows)]
            k = 2 * block + part
            moves.append(
                (
                    pltpu.make_async_copy(source.at[block, here], held.at[block, here], sem_in.at[k]),
                    pltpu.make_async_copy(wide.at[block, here], target, sem_out.at[k]), block, here,
                )
            )
    for fetch, store, block, here in moves:
        fetch.start()
    yield
    for fetch, store, block, here in moves:
        fetch.wait()
        for o in range(0, rows, COPY):
            at = pl.ds(here.start + o, COPY)
            wide[block, at, :] = held[block, at, :].astype(F32)
        store.start()
    yield
    for fetch, store, block, here in moves:
        store.wait()


def finish_far(far_in, dmi_in, dmo_in, dmi_hbm, dmo_hbm, far_v, far_f, sem_in, sem_out):
    side = 1 - lax.rem(lax.axis_index("batch"), 2)
    for _ in widen(far_in, far_v, far_f, dmi_hbm, dmo_hbm, side, sem_in, sem_out):
        pass


def local(
    batch, grid,
    inputs, cotangent, dataset_ids, channel_masks, sample_counts, norm1_gain, norm1_bias,
    spec_w1, spec_b1, spec_w2, spec_b2, norm2_gain, norm2_bias, mlp_in, mlp_in_bias, mlp_out, mlp_out_bias,
):
    items, rows, cols, feats = inputs.shape
    hidden = mlp_in.shape[1]
    sz = sizes_of(items, rows, cols, feats, hidden, grid)
    batch_bits, grid_bits = batch.bit_length() - 1, grid.bit_length() - 1
    bits = batch_bits + grid_bits

    vmem = pl.BlockSpec(memory_space=pltpu.VMEM)
    smem = pl.BlockSpec(memory_space=pltpu.SMEM)
    hbm = pl.BlockSpec(memory_space=pl.ANY)
    chunks, groups, blocks = sz.chunks, feats // 128, hidden // FT
    shape = (chunks, CELLS, feats)
    pieces = (chunks, grid, sz.subs, 16, feats)
    seg_rows = 2 * feats
    mix_rows = 4 * groups * BSIZE
    late = (grid, mix_rows // (2 * grid) + 16, 128)
    plane, planes = sz.plane, sz.planes
    out_shape = (
        jax.ShapeDtypeStruct(shape, BF16),
        jax.ShapeDtypeStruct(shape, F32),
        jax.ShapeDtypeStruct((blocks, feats, FT), BF16),
        jax.ShapeDtypeStruct((2, mix_rows // 2, 128), BF16),
        jax.ShapeDtypeStruct((16, feats), F32),
    )
    dma = pltpu.SemaphoreType.DMA
    scratch = [
        pltpu.VMEM(shape, BF16),
        pltpu.VMEM(shape, BF16),
        pltpu.VMEM(mlp_in.shape, BF16),
        pltpu.VMEM(mlp_out.shape, BF16),
        *[pltpu.VMEM(pieces, BF16)] * 4,
        pltpu.VMEM(shape, F32),
        pltpu.VMEM((chunks, 2, sz.modes, feats), BF16),
        pltpu.VMEM((chunks, sz.modes, 2 * feats), BF16),
        pltpu.VMEM((chunks, sz.modes, 2 * feats), F32),
        pltpu.VMEM((chunks, sz.modes, 2 * feats), F32),
        pltpu.VMEM((groups, 256, 256), BF16),
        pltpu.VMEM((groups, 256, 256), BF16),
        pltpu.VMEM((groups, 256, 256), F32),
        pltpu.VMEM((groups, 256, 256), F32),
        pltpu.VMEM((CELLS, feats), BF16),
        pltpu.VMEM((feats, CELLS), BF16),
        pltpu.VMEM((CELLS, feats), BF16),
        pltpu.VMEM((feats, CELLS), BF16),
        pltpu.VMEM((CELLS, hidden), BF16),
        pltpu.VMEM((CELLS, hidden), BF16),
        pltpu.VMEM((items, 1, feats), F32),
        pltpu.VMEM((items, 1, feats), F32),
        pltpu.VMEM((blocks, seg_rows, FT), F32),
        pltpu.VMEM((blocks, landing_rows(seg_rows, bits), FT), BF16),
        pltpu.VMEM((2, *late), F32),
        pltpu.VMEM((batch_bits, *late), BF16),
        pltpu.VMEM((batch_bits, *late), BF16),
        pltpu.VMEM((planes, plane, *late[1:]), BF16),
        pltpu.VMEM((plane, planes, *late[1:]), BF16),
        pltpu.VMEM((planes, *late[1:]), BF16),
        pltpu.VMEM((planes, *late[1:]), BF16),
        *[pltpu.VMEM((planes, plane, *late[1:]), BF16)] * 2,
        pltpu.VMEM((16, feats), F32),
        pltpu.VMEM((16, 8, feats), F32),
        pltpu.VMEM((CELLS, FT), F32),
        pltpu.VMEM((CELLS, FT), F32),
        pltpu.VMEM((2, 2 * groups, 128), F32),
        pltpu.VMEM((batch * plane, 2 * groups, 128), F32),
        pltpu.VMEM((planes, 2 * groups, 128), F32),
        dma((chunks,)),
        dma((chunks,)),
        dma((2,)),
        dma((chunks,)),
        dma((chunks,)),
        dma((blocks,)),
        *[dma((4, chunks))] * 2,
        dma((blocks, 2 * bits)),
        dma((blocks, 2 * bits)),
        dma((batch_bits + 5,)),
        dma((batch_bits + 5,)),
        dma((2,)),
        dma((2,)),
    ]
    cells = items * rows * cols
    row = lambda v: v.reshape(1, -1)
    parts = pl.pallas_call(
        functools.partial(kernel, sz, batch_bits, grid_bits),
        out_shape=out_shape,
        in_specs=[smem] * 3 + [hbm, hbm] + [vmem] * 14 + [hbm, hbm],
        out_specs=(hbm, hbm, hbm, vmem, vmem),
        scratch_shapes=scratch,
        cost_estimate=pl.CostEstimate(
            flops=14 * cells * feats * hidden, bytes_accessed=24 << 20, transcendentals=3 * cells * hidden
        ),
        compiler_params=pltpu.CompilerParams(
            collective_id=0, has_side_effects=True, vmem_limit_bytes=67_000_000
        ),
    )(
        dataset_ids, channel_masks.T, sample_counts,
        inputs.reshape(shape), cotangent.reshape(shape),
        row(norm1_gain), row(norm1_bias), row(norm2_gain), row(norm2_bias),
        spec_w1, spec_b1, spec_w2, spec_b2, row(mlp_in_bias), row(mlp_out_bias),
        *[jnp.asarray(t) for t in tables(sz)], mlp_in, mlp_out,
    )
    vector = jax.ShapeDtypeStruct((1, feats), F32)
    pair = jax.ShapeDtypeStruct((2, feats), F32)
    mixers = jax.ShapeDtypeStruct(spec_w1.shape, F32)
    moves = 2 * blocks + 2 * chunks
    half_shape = (blocks, feats, FT)
    outs = pl.pallas_call(
        functools.partial(finish, sz),
        out_shape=(
            out_shape[0], out_shape[1], vector, vector, mixers, pair, mixers, pair, vector, vector,
            jax.ShapeDtypeStruct(mlp_in.shape, F32), jax.ShapeDtypeStruct((1, hidden), F32),
            jax.ShapeDtypeStruct(mlp_out.shape, F32), vector,
        ),
        in_specs=[hbm] * 5,
        out_specs=(hbm, hbm) + (vmem,) * 8 + (hbm, vmem, hbm, vmem),
        scratch_shapes=[
            pltpu.VMEM(shape, BF16), pltpu.VMEM(shape, F32), pltpu.VMEM(half_shape, BF16), pltpu.VMEM(half_shape, F32),
            pltpu.VMEM(out_shape[3].shape, BF16), pltpu.VMEM(out_shape[4].shape, F32),
            dma((moves,)), dma((moves,)), dma((2,)),
        ],
        cost_estimate=pl.CostEstimate(flops=0, bytes_accessed=24 << 20, transcendentals=0),
        compiler_params=pltpu.CompilerParams(vmem_limit_bytes=67_000_000),
    )(*parts)
    far = lax.ppermute(parts[2], "batch", [(b, b ^ 1) for b in range(batch)])
    wide = (jax.ShapeDtypeStruct(mlp_in.shape, F32), jax.ShapeDtypeStruct(mlp_out.shape, F32))
    dmi, dmo = pl.pallas_call(
        finish_far,
        out_shape=wide,
        in_specs=[hbm] * 3,
        out_specs=(hbm, hbm),
        input_output_aliases={1: 0, 2: 1},
        scratch_shapes=[
            pltpu.VMEM(half_shape, BF16), pltpu.VMEM(half_shape, F32), dma((2 * blocks,)), dma((2 * blocks,)),
        ],
        cost_estimate=pl.CostEstimate(flops=0, bytes_accessed=6 << 20, transcendentals=0),
        compiler_params=pltpu.CompilerParams(vmem_limit_bytes=67_000_000),
    )(far, outs[10], outs[12])
    flat = lambda v: v.reshape(-1)
    return (
        outs[0].reshape(inputs.shape), outs[1].reshape(inputs.shape), flat(outs[2]), flat(outs[3]), *outs[4:8],
        flat(outs[8]), flat(outs[9]), dmi, flat(outs[11]), dmo, flat(outs[13]),
    )


def solution(mesh):
    spread = P("batch", "grid", None, None)
    return jax.shard_map(
        functools.partial(local, mesh.shape["batch"], mesh.shape["grid"]),
        mesh=mesh,
        in_specs=(spread, spread, P("batch")) + (P(),) * 14,
        out_specs=(spread, spread) + (P(),) * 12,
        check_vma=False,
    )
```
